32 devices in a mesh: samp: 8 (over z, y), head: 4 (over x, core).
Axes of the slice: x: 2, y: 2, z: 4, core: 2. Of those that a mesh axis runs over, the one named last changes fastest.
Arguments:
- queries: bfloat16 [8, 768, 512], P('samp', 'head'), may hold values from -10 to 10
- keys: bfloat16 [8, 768, 512], P('samp', 'head'), may hold values from -10 to 10
- values: bfloat16 [8, 768, 512], P('samp', 'head'), may hold values from -6 to 6
- out_grad: bfloat16 [8, 768, 512], P('samp', 'head'), may hold values from -6 to 6
- pair: bfloat16 [512, 512, 128], P('head', 'samp'), may hold values from -6 to 6
- ln_gain: float32 [128], replicated, may hold values from 0.25 to 1.75
- proj_weight: bfloat16 [128, 16], replicated, may hold values from -0.5 to 0.5
- token_mask: int32 [512], replicated, may hold values from 0 to 1, as said below
- atom_map: int32 [4096], replicated, may hold values from 0 to 511, never falling along the last dimension, each value on 1 to 24 neighbouring positions
Outputs:
- attended: bfloat16 [8, 768, 512], P('samp', 'head')
- query_grad: bfloat16 [8, 768, 512], P('samp', 'head')
- key_grad: bfloat16 [8, 768, 512], P('samp', 'head')
- value_grad: bfloat16 [8, 768, 512], P('samp', 'head')
- pair_grad: bfloat16 [512, 512, 128], P('head', 'samp')
- weight_grad: float32 [128, 16], replicated
- gain_grad: float32 [128], replicated
The draws below stay inside these ranges and needn't reach their ends.
Inputs may be any that keep to these rules, and one draw needn't show every extreme that they name: `token_mask`: real tokens form a prefix of 256 or more tokens; the last token is padding.
All inputs are finite; a program needn't handle non-finite values.
Results may differ from the reference program's by a relative error of at most 0.02.
Values may be sent and summed in bfloat16 or wider, within the bound.
No kernel may reach another device: no remote copies, remote signals or barrier semaphores. Data moves between devices by JAX's collectives and lax.ppermute only.
A program may use at most 64 MiB of HBM per device.

```python
import math
import jax
import jax.numpy as jnp
import numpy as np
from jax import lax

N = 512
D = 768
HEADS = 16
D_PAIR = 128
ATOM_MOST = 24
SAMPLES = 8
ATOMS = 4096


def drawn_pair(key):
    base = jax.random.fold_in(key, 11)
    key_query, key_keys = jax.random.split(base, 2)
    shape = (SAMPLES, N, D)
    query_all = jnp.clip(jax.random.normal(key_query, shape, jnp.float32), -6.0, 6.0)
    keys_all = jnp.clip(jax.random.normal(key_keys, shape, jnp.float32), -6.0, 6.0)
    return (jnp.swapaxes(query_all, 1, 2), jnp.swapaxes(keys_all, 1, 2))


def draw_queries(key, part):
    return drawn_pair(key)[0].astype(jnp.bfloat16)


def draw_keys(key, part):
    return drawn_pair(key)[1].astype(jnp.bfloat16)


def draw_token_mask(key, part):
    length = jax.random.randint(jax.random.fold_in(key, 23), (), N // 2, N)
    return (jnp.arange(N) < length).astype(jnp.int32)


def shard_levels(stream_key, shape, cuts, low, top_value):
    def one(dim, shards_of):
        draws = jax.random.uniform(jax.random.fold_in(jax.random.fold_in(stream_key, 6), dim), (shards_of,), jnp.float32, low / len(cuts), top_value / len(cuts))
        return jnp.repeat(jnp.exp(draws), shape[dim] // shards_of).reshape((-1,) + (1,) * (len(shape) - dim - 1))

    loudness = one(*cuts[0])
    for cut in cuts[1:]:
        loudness = loudness * one(*cut)
    return loudness


def split_up(count, total, limit, lean):
    loads = [(1 << 20) // math.isqrt(rank ** lean) + 1 for rank in range(2, count + 1)]
    rest, given = total - limit - (count - 1), [1] * (count - 1)
    while rest > 0:
        movable = [i for i in range(count - 1) if given[i] < limit]
        pool, budget = sum([loads[i] for i in movable]), rest
        for i in movable:
            extra = min(limit - given[i], max(1, budget * loads[i] // pool), rest)
            given[i] = given[i] + extra
            rest = rest - extra
    return np.array([limit] + given)


def ragged(stream_key, number_of, total, reach, slope):
    if number_of == 2:
        one = jax.random.randint(stream_key, (), max(1, total - reach), min(reach, total - 1) + 1)
        return jnp.stack([one, total - one])
    sizes = jnp.asarray(split_up(number_of, total, reach, slope), jnp.int32)
    twos = (number_of - 1) // 2
    donor, taker = sizes[1:1 + 2 * twos:2], sizes[2:2 + 2 * twos:2]
    slack = jnp.minimum(donor - 1, reach - taker)
    moved = jax.random.randint(jax.random.fold_in(stream_key, 1), (twos,), 0, 1 << 20) % (slack + 1)
    sizes = sizes.at[1:1 + 2 * twos:2].set(donor - moved).at[2:2 + 2 * twos:2].set(taker + moved)
    return sizes[jax.random.permutation(jax.random.fold_in(stream_key, 2), number_of)]


def centred(key, extent, deviation, reach, pieces=(), kind=jnp.bfloat16):
    values = deviation * jax.random.normal(key, extent, jnp.float32)
    if pieces:
        values = values * shard_levels(key, extent, pieces, -0.22, 0.18)
    return jnp.clip(values, -reach, reach).astype(kind)


def setup_inputs(seed: int = 0) -> dict:
    seeds = jax.random.split(jax.random.key(seed), 10)
    return {
        "queries": draw_queries(jax.random.fold_in(seeds[9], 71), 0),
        "keys": draw_keys(jax.random.fold_in(seeds[9], 71), 0),
        "values": centred(seeds[2], (SAMPLES, D, N), 1.0, 6.0, ((0, 8), (1, 4))),
        "out_grad": centred(seeds[3], (SAMPLES, D, N), 1.0, 6.0, ((0, 8), (1, 4))),
        "pair": centred(seeds[4], (N, N, D_PAIR), 1.0, 6.0, ((0, 4), (1, 8))),
        "ln_gain": jnp.clip(1.0 + 0.15 * jax.random.normal(seeds[5], (D_PAIR,), jnp.float32), 0.25, 1.75),
        "proj_weight": centred(seeds[6], (D_PAIR, HEADS), D_PAIR ** -0.5, 0.5),
        "token_mask": draw_token_mask(jax.random.fold_in(seeds[9], 71), 0),
        "atom_map": jnp.searchsorted(jnp.cumsum(ragged(seeds[8], N, ATOMS, ATOM_MOST, 2)), jnp.arange(ATOMS), side="right").astype(jnp.int32),
    }


def token_weights(atom_map, token_mask):
    count = token_mask.shape[0]
    ends = jnp.searchsorted(atom_map, jnp.arange(count, dtype=jnp.int32), side='right').astype(jnp.int32)
    starts = jnp.concatenate([jnp.zeros((1,), jnp.int32), ends[:-1]])
    return (ends - starts).astype(jnp.float32) * (count / atom_map.shape[0]) * token_mask.astype(jnp.float32)

def layer_norm(pair, ln_gain):
    wide = pair.astype(jnp.float32)
    center = lax.optimization_barrier(jnp.mean(wide, axis=-1, keepdims=True))
    spread = lax.optimization_barrier(jnp.mean(jnp.square(wide - center), axis=-1, keepdims=True))
    inv_std = 1.0 / jnp.sqrt(spread + 1e-05)
    normed = (wide - center) * inv_std
    lnout = (normed * ln_gain).astype(jnp.bfloat16)
    return (normed, inv_std, lnout)

def attend(query_row, key_row, value_row, grad_row, bias, key_keep, tok_weight):
    count = query_row.shape[1]
    local_heads = bias.shape[0]
    query_h = query_row.reshape(local_heads, -1, count).astype(jnp.float32)
    key_h = key_row.reshape(local_heads, -1, count).astype(jnp.float32)
    value_h = value_row.reshape(local_heads, -1, count).astype(jnp.float32)
    inv_root = 1.0 / jnp.sqrt(jnp.float32(query_h.shape[1]))
    scores = jnp.einsum('hdi,hdj->hij', query_h, key_h) * inv_root + bias.astype(jnp.float32)
    scores = jnp.where(key_keep[None, None, :], scores, jnp.float32(-1000000000.0))
    largest = lax.optimization_barrier(jnp.max(scores, axis=-1, keepdims=True))
    expo = jnp.exp(scores - largest)
    prob = expo / lax.optimization_barrier(jnp.sum(expo, axis=-1, keepdims=True))
    prob_b = prob.astype(jnp.bfloat16).astype(jnp.float32)
    attended = jnp.einsum('hij,hdj->hdi', prob_b, value_h).astype(jnp.bfloat16)
    grad_in = (grad_row.astype(jnp.float32) * tok_weight[None, :]).astype(jnp.bfloat16)
    grad_h = grad_in.reshape(local_heads, -1, count).astype(jnp.float32)
    dprob = jnp.einsum('hdi,hdj->hij', grad_h, value_h)
    row_dot = lax.optimization_barrier(jnp.sum(prob * dprob, axis=-1, keepdims=True))
    dscore = prob * (dprob - row_dot)
    dscore_b = dscore.astype(jnp.bfloat16).astype(jnp.float32)
    query_grad = (jnp.einsum('hij,hdj->hdi', dscore_b, key_h) * inv_root).astype(jnp.bfloat16)
    key_grad = (jnp.einsum('hij,hdi->hdj', dscore_b, query_h) * inv_root).astype(jnp.bfloat16)
    value_grad = jnp.einsum('hij,hdi->hdj', prob_b, grad_h).astype(jnp.bfloat16)
    shape = (-1, count)
    return (attended.reshape(shape), query_grad.reshape(shape), key_grad.reshape(shape), value_grad.reshape(shape), dscore.astype(jnp.float32))

def reference(queries, keys, values, out_grad, pair, ln_gain, proj_weight, token_mask, atom_map):
    count = pair.shape[0]
    key_keep = token_mask > 0
    tok_weight = token_weights(atom_map, token_mask)
    normed, inv_std, lnout = layer_norm(pair, ln_gain)
    bias = jnp.einsum('ijc,ch->hij', lnout.astype(jnp.float32), proj_weight.astype(jnp.float32)).astype(jnp.bfloat16)

    def one_sample(total, items):
        query_row, key_row, value_row, grad_row = items
        attended, query_grad, key_grad, value_grad, dscore = attend(query_row, key_row, value_row, grad_row, bias, key_keep, tok_weight)
        return (total + dscore, (attended, query_grad, key_grad, value_grad))
    start = jnp.zeros(bias.shape, jnp.float32)
    bias_grad, outs = lax.scan(one_sample, start, (queries, keys, values, out_grad))
    attended, query_grad, key_grad, value_grad = outs
    highest = lax.Precision.HIGHEST
    lnout_grad = jnp.einsum('hij,ch->ijc', bias_grad, proj_weight.astype(jnp.float32), precision=highest)
    weight_grad = jnp.einsum('ijc,hij->ch', lnout.astype(jnp.float32), bias_grad, precision=highest) / count
    gain_grad = lax.optimization_barrier(jnp.sum(lnout_grad * normed, axis=(0, 1))) / count
    scaled = lnout_grad * ln_gain
    pair_grad = (scaled - lax.optimization_barrier(jnp.mean(scaled, axis=-1, keepdims=True)) - normed * lax.optimization_barrier(jnp.mean(scaled * normed, axis=-1, keepdims=True))) * inv_std
    return (attended, query_grad, key_grad, value_grad, pair_grad.astype(jnp.bfloat16), weight_grad, gain_grad)
```

```python
import functools
import math

import jax
import jax.numpy as jnp
from jax import lax
from jax.experimental import pallas as pl
from jax.experimental.pallas import tpu as pltpu
from jax.sharding import Mesh
from jax.sharding import PartitionSpec as P

F32 = jnp.float32
BF16 = jnp.bfloat16
LOG2E = math.log2(math.e)
EPS = 1e-05
MASKED = -1000000000.0
PARAMS = pltpu.CompilerParams(vmem_limit_bytes=48 * 1024 * 1024)
NT = (((1,), (1,)), ((), ()))
TN = (((0,), (0,)), ((), ()))


def dot(a, b, dims=(((1,), (0,)), ((), ()))):
    return lax.dot_general(a, b, dims, preferred_element_type=F32)


def call(kernel, name, flops, moved, **kw):
    return pl.pallas_call(
        kernel,
        name=name,
        compiler_params=PARAMS,
        cost_estimate=pl.CostEstimate(flops=flops, bytes_accessed=moved, transcendentals=0),
        **kw,
    )


def step_of(count, most):
    return max(n for n in range(1, most + 1) if count % n == 0)


def pack_kernel(mates, dim, q_ref, k_ref, v_ref, g_ref, map_ref, mask_ref, send_ref):
    count = mask_ref.shape[1]
    atoms = map_ref.shape[1]
    rows = pl.cdiv(count, 128)
    tall = pl.cdiv(rows, 16) * 16
    token = map_ref[...]
    high = lax.shift_right_logical(token, 7)
    low = jnp.bitwise_and(token, 127)
    is_row = (lax.broadcasted_iota(jnp.int32, (tall, atoms), 0) == high).astype(F32).astype(BF16)
    is_lane = (lax.broadcasted_iota(jnp.int32, (128, atoms), 0) == low).astype(F32).astype(BF16)
    counts = dot(is_row, is_lane, NT)
    line = jnp.concatenate([counts[r : r + 1, :] for r in range(rows)], axis=1)[:, :count]
    weight = line * (count / atoms) * mask_ref[...].astype(F32)
    for m in range(mates):
        part = pl.ds(m * dim, dim)
        send_ref[m, 0:dim, :] = q_ref[0, part, :]
        send_ref[m, dim : 2 * dim, :] = k_ref[0, part, :]
        send_ref[m, 2 * dim : 3 * dim, :] = v_ref[0, part, :]
        send_ref[m, 3 * dim : 4 * dim, :] = (g_ref[0, part, :].astype(F32) * weight).astype(BF16)


def unpack_kernel(mates, dim, got_ref, *out_refs):
    for m in range(mates):
        for n, out_ref in enumerate(out_refs):
            out_ref[0, pl.ds(m * dim, dim), :] = got_ref[m, n * dim : (n + 1) * dim, :]


def norm_kernel(groups, mates, pair_ref, gain_ref, proj_ref, cent_ref, send_ref, inv_ref, bias_s, var_s):
    step = pl.program_id(0)
    block, cols, chan = pair_ref.shape
    heads = proj_ref.shape[0]
    rows = var_s.shape[0]
    wide = pair_ref[...].astype(F32).reshape(block * cols, chan)
    cent = wide - jnp.mean(wide, axis=-1, keepdims=True)
    square = cent * cent
    inv_std = lax.rsqrt(jnp.mean(square, axis=-1, keepdims=True) + EPS)
    lnout = (cent * inv_std * gain_ref[...]).astype(BF16)
    cent_ref[...] = cent.astype(BF16).reshape(block, cols, chan)
    square = square.astype(BF16)
    ones = jnp.full((16, chan), 1.0, BF16)
    for a in range(block):
        part = slice(a * cols, (a + 1) * cols)
        bias_s[pl.ds(step * block + a, heads, stride=rows), :] = dot(proj_ref[...], lnout[part], NT)
        var_s[pl.ds(step * block + a, 1), :] = dot(ones, square[part], NT)[:1] * (1.0 / chan)

    @pl.when(step == pl.num_programs(0) - 1)
    def _():
        inv_ref[...] = lax.rsqrt(var_s[...].T + EPS)
        local = send_ref.shape[0] // (groups * mates)
        for h in range(heads):
            block_t = bias_s[h * rows : (h + 1) * rows, :].T.astype(BF16)
            owner, mate = h // mates, h % mates
            for g in range(groups):
                send_ref[(g * mates + mate) * local + owner] = block_t


def attend_kernel(wide, got_ref, bias_ref, mask_ref, back_ref, grad_ref, key_s, value_s, dk_s, dv_s):
    samples, four, count = got_ref.shape
    dim = four // 4
    root = 1.0 / math.sqrt(dim)
    samp, heads, cols, rows = bias_ref.shape
    first = lax.broadcasted_iota(jnp.int32, (16, count), 0) == 0
    mask_rows = jnp.where(first & (mask_ref[...] <= 0), MASKED, 0.0).astype(BF16)
    one_rows = jnp.where(lax.broadcasted_iota(jnp.int32, (16, wide), 0) == 0, 1.0, 0.0).astype(BF16)
    for s in range(samples):
        keys = got_ref[s, dim : 2 * dim, :]
        key_s[s] = jnp.concatenate([keys, keys, mask_rows], axis=0).T
        value_s[s] = got_ref[s, 2 * dim : 3 * dim, :].T
    per = wide // rows
    for a in range(count // wide):
        lanes = slice(a * wide, (a + 1) * wide)
        bias = jnp.concatenate(
            [bias_ref[:, a * per + p].reshape(count, rows) for p in range(per)], axis=1
        ).astype(F32) * LOG2E
        total = None
        for s in range(samples):
            query = got_ref[s, 0:dim, lanes]
            scaled = query.astype(F32) * (LOG2E * root)
            upper = scaled.astype(BF16)
            lower = (scaled - upper.astype(F32)).astype(BF16)
            scores = dot(key_s[s], jnp.concatenate([upper, lower, one_rows], axis=0)) + bias
            expo = jnp.exp2(scores - jnp.max(scores, axis=0, keepdims=True))
            inv_sum = 1.0 / jnp.sum(expo, axis=0, keepdims=True)
            expo_b = expo.astype(BF16)
            out = dot(got_ref[s, 2 * dim : 3 * dim, :], expo_b) * inv_sum
            back_ref[s, 0:dim, lanes] = out.astype(BF16)
            grad = (got_ref[s, 3 * dim : 4 * dim, lanes].astype(F32) * inv_sum).astype(BF16)
            row_dot = jnp.sum(grad.astype(F32) * out, axis=0, keepdims=True)
            dscore = expo * (dot(value_s[s], grad) - row_dot)
            total = dscore if total is None else total + dscore
            dscore_b = dscore.astype(BF16)
            back_ref[s, dim : 2 * dim, lanes] = (
                dot(got_ref[s, dim : 2 * dim, :], dscore_b) * root
            ).astype(BF16)
            dk = dot(query, dscore_b, NT)
            dv = dot(grad, expo_b, NT)
            if a == 0:
                dk_s[s] = dk
                dv_s[s] = dv
            else:
                dk_s[s] += dk
                dv_s[s] += dv
        total = total.astype(BF16)
        for p in range(per):
            grad_ref[:, a * per + p] = total[:, p * rows : (p + 1) * rows].reshape(samp, cols, rows)
    for s in range(samples):
        back_ref[s, 2 * dim : 3 * dim, :] = (dk_s[s] * root).astype(BF16)
        back_ref[s, 3 * dim : 4 * dim, :] = dv_s[s].astype(BF16)


def reduce_kernel(groups, mates, got_ref, bias_ref, inv_ref, cent_ref, left_ref, sum_ref, plain_s, biased_s):
    step = pl.program_id(0)
    block, cols, chan = cent_ref.shape
    rows = inv_ref.shape[1]
    heads = sum_ref.shape[0]
    local = heads // mates

    @pl.when(step == 0)
    def _():
        sum_ref[...] = jnp.zeros_like(sum_ref)
        inv_std = inv_ref[...]
        for h in range(heads):
            at = (h % mates) * local + h // mates
            grad = got_ref[at].astype(F32)
            for g in range(1, groups):
                grad += got_ref[g * heads + at].astype(F32)
            plain = grad * inv_std
            biased = plain * inv_std * bias_ref[at].astype(F32) * (1.0 / chan)
            plain_s[h * rows : (h + 1) * rows, :] = plain.T
            biased_s[h * rows : (h + 1) * rows, :] = biased.T

    total = sum_ref[...]
    for a in range(block):
        take = pl.ds(step * block + a, heads, stride=rows)
        plain = plain_s[take, :].astype(BF16)
        left_ref[a, 0:heads, :] = plain
        left_ref[a, heads : 2 * heads, :] = biased_s[take, :].astype(BF16)
        total += dot(plain, cent_ref[a])
    sum_ref[...] = total


def pair_kernel(left_ref, right_ref, cent_ref, out_ref):
    block, cols, chan = cent_ref.shape
    for a in range(block):
        both = dot(left_ref[a], right_ref[...], TN)
        out_ref[a] = (both[:, :chan] - cent_ref[a].astype(F32) * both[:, chan:]).astype(BF16)


def final_kernel(scale, sums_ref, gain_ref, proj_ref, weight_ref, gain_grad_ref):
    total = sums_ref[0].astype(F32)
    for n in range(1, sums_ref.shape[0]):
        total += sums_ref[n].astype(F32)
    total = total * scale
    weight_ref[...] = (total * gain_ref[...]).T
    gain_grad_ref[...] = jnp.sum(total * proj_ref[...], axis=0, keepdims=True)


def local(groups, mates, axes, queries, keys, values, out_grad, pair, ln_gain, proj_weight, token_mask, atom_map):
    _, width, count = queries.shape
    rows, cols, chan = pair.shape
    heads = proj_weight.shape[1]
    dim = width // mates
    head_parts = heads // mates
    devices = groups * mates * head_parts
    entries = rows * cols
    gain_row = ln_gain.reshape(1, chan)
    proj_rows = proj_weight.T
    mask_row = token_mask.reshape(1, count)
    whole = lambda *shape: pl.BlockSpec(shape, lambda *_: (0,) * len(shape))

    chunks = jax.ShapeDtypeStruct((mates, 4 * dim, count), BF16)
    tiles = jax.ShapeDtypeStruct((devices, cols, rows), BF16)
    send = call(
        functools.partial(pack_kernel, mates, dim), "pack", 2 * 16 * 128 * atom_map.shape[0],
        16 * width * count, out_shape=chunks,
    )(queries, keys, values, out_grad, atom_map.reshape(1, -1), mask_row)
    got = lax.all_to_all(send, axes[1], 0, 0, tiled=True) if mates > 1 else send

    block = step_of(rows, 16)
    cent, bias_send, inv_std = call(
        functools.partial(norm_kernel, groups, mates), "norm", 2 * entries * chan * heads,
        4 * entries * chan,
        out_shape=(
            jax.ShapeDtypeStruct((rows, cols, chan), BF16),
            tiles,
            jax.ShapeDtypeStruct((cols, rows), F32),
        ),
        grid=(rows // block,),
        in_specs=[
            pl.BlockSpec((block, cols, chan), lambda i: (i, 0, 0)),
            whole(1, chan),
            whole(heads, chan),
        ],
        out_specs=(
            pl.BlockSpec((block, cols, chan), lambda i: (i, 0, 0)),
            whole(devices, cols, rows),
            whole(cols, rows),
        ),
        scratch_shapes=[pltpu.VMEM((heads * rows, cols), F32), pltpu.VMEM((rows, cols), F32)],
    )(pair, gain_row, proj_rows)
    bias = lax.all_to_all(bias_send, axes, 0, 0, tiled=True)

    fine = rows % 128 == 0
    samp = groups * mates
    if fine:
        bias = bias.reshape(samp, head_parts, cols, rows)
    else:
        bias = bias.reshape(samp, head_parts, cols, rows).transpose(0, 2, 1, 3)
        bias = bias.reshape(1, 1, count, count)
    wide = max(bias.shape[3], step_of(count, 256)) if fine else count
    back, grads = call(
        functools.partial(attend_kernel, wide), "attend", 12 * mates * dim * count * count,
        8 * mates * dim * count * 2 + 4 * count * count,
        out_shape=(chunks, jax.ShapeDtypeStruct(bias.shape, BF16)),
        scratch_shapes=[
            pltpu.VMEM((mates, count, 2 * dim + 16), BF16),
            pltpu.VMEM((mates, count, dim), BF16),
            pltpu.VMEM((mates, dim, count), F32),
            pltpu.VMEM((mates, dim, count), F32),
        ],
    )(got, bias, mask_row)
    if not fine:
        grads = grads.reshape(samp, cols, head_parts, rows).transpose(0, 2, 1, 3)
    grads = lax.all_to_all(grads.reshape(devices, cols, rows), axes, 0, 0, tiled=True)
    outs = lax.all_to_all(back, axes[1], 0, 0, tiled=True) if mates > 1 else back
    attended, query_grad, key_grad, value_grad = call(
        functools.partial(unpack_kernel, mates, dim), "unpack", 0, 16 * width * count,
        out_shape=(jax.ShapeDtypeStruct(queries.shape, BF16),) * 4,
    )(outs)

    left, part = call(
        functools.partial(reduce_kernel, groups, mates), "reduce", 2 * entries * chan * heads,
        2 * entries * chan,
        out_shape=(
            jax.ShapeDtypeStruct((rows, 2 * heads, cols), BF16),
            jax.ShapeDtypeStruct((heads, chan), F32),
        ),
        grid=(rows // block,),
        in_specs=[
            whole(devices, cols, rows),
            whole(heads, cols, rows),
            whole(cols, rows),
            pl.BlockSpec((block, cols, chan), lambda i: (i, 0, 0)),
        ],
        out_specs=(
            pl.BlockSpec((block, 2 * heads, cols), lambda i: (i, 0, 0)),
            whole(heads, chan),
        ),
        scratch_shapes=[pltpu.VMEM((heads * rows, cols), F32)] * 2,
    )(grads, bias_send, inv_std, cent)
    parts = jnp.broadcast_to(part[None], (devices, heads, chan))
    sums = lax.all_to_all(parts, axes, 0, 0, tiled=True)

    scaled = proj_rows.astype(F32) * gain_row
    scaled = scaled - jnp.mean(scaled, axis=1, keepdims=True)
    none = jnp.zeros_like(scaled)
    right = jnp.concatenate(
        [jnp.concatenate([scaled, none], axis=1), jnp.concatenate([none, none + 1.0], axis=1)], axis=0
    ).astype(BF16)
    pair_grad = call(
        pair_kernel, "pair_grad", 2 * entries * chan * heads * 4, 4 * entries * chan,
        out_shape=jax.ShapeDtypeStruct(pair.shape, BF16),
        grid=(rows // block,),
        in_specs=[
            pl.BlockSpec((block, 2 * heads, cols), lambda i: (i, 0, 0)),
            whole(2 * heads, 2 * chan),
            pl.BlockSpec((block, cols, chan), lambda i: (i, 0, 0)),
        ],
        out_specs=pl.BlockSpec((block, cols, chan), lambda i: (i, 0, 0)),
    )(left, right, cent)
    weight_grad, gain_grad = call(
        functools.partial(final_kernel, 1.0 / count), "final", 0, 4 * devices * heads * chan,
        out_shape=(
            jax.ShapeDtypeStruct((chan, heads), F32),
            jax.ShapeDtypeStruct((1, chan), F32),
        ),
    )(sums, gain_row, proj_rows.astype(F32))
    return attended, query_grad, key_grad, value_grad, pair_grad, weight_grad, gain_grad.reshape(chan)


def solution(mesh):
    samp, head = mesh.axis_names
    samp_size, head_size = mesh.shape[samp], mesh.shape[head]

    def run(*args):
        heads = args[6].shape[1]
        mates = math.gcd(heads // head_size, samp_size)
        groups = samp_size // mates
        axes = ("group", "mate", "part")
        fine = Mesh(mesh.devices.reshape(groups, mates, head_size), axes)
        by_sample = P(("group", "mate"), "part", None)
        by_pair = P("part", ("group", "mate"), None)
        return jax.shard_map(
            functools.partial(local, groups, mates, axes),
            mesh=fine,
            in_specs=(by_sample,) * 4 + (by_pair,) + (P(),) * 4,
            out_specs=(by_sample,) * 4 + (by_pair, P(), P()),
            check_vma=False,
        )(*args)

    return run
```

```python
import functools
import math

import jax
import jax.numpy as jnp
from jax import lax
from jax.experimental import pallas as pl
from jax.experimental.pallas import tpu as pltpu
from jax.sharding import Mesh
from jax.sharding import PartitionSpec as P

F32 = jnp.float32
BF16 = jnp.bfloat16
LOG2E = math.log2(math.e)
EPS = 1e-05
MASKED = -1000000000.0
BIG = 60
NT = (((1,), (1,)), ((), ()))
TN = (((0,), (0,)), ((), ()))


def dot(a, b, dims=(((1,), (0,)), ((), ()))):
    return lax.dot_general(a, b, dims, preferred_element_type=F32)


def call(kernel, name, flops, moved, mebi, **kw):
    return pl.pallas_call(
        kernel,
        name=name,
        compiler_params=pltpu.CompilerParams(vmem_limit_bytes=mebi * 1024 * 1024),
        cost_estimate=pl.CostEstimate(flops=flops, bytes_accessed=moved, transcendentals=0),
        **kw,
    )


def step_of(count, most):
    return max(n for n in range(1, most + 1) if count % n == 0)


def pack_kernel(dim, mate_ref, q_ref, k_ref, v_ref, g_ref, map_ref, mask_ref, *send_refs):
    count = mask_ref.shape[1]
    atoms = map_ref.shape[1]
    rows = pl.cdiv(count, 128)
    tall = pl.cdiv(rows, 16) * 16
    token = map_ref[...]
    high = lax.shift_right_logical(token, 7)
    low = jnp.bitwise_and(token, 127)
    is_row = (lax.broadcasted_iota(jnp.int32, (tall, atoms), 0) == high).astype(F32).astype(BF16)
    is_lane = (lax.broadcasted_iota(jnp.int32, (128, atoms), 0) == low).astype(F32).astype(BF16)
    counts = dot(is_row, is_lane, NT)
    line = jnp.concatenate([counts[r : r + 1, :] for r in range(rows)], axis=1)[:, :count]
    weight = line * (count / atoms) * mask_ref[...].astype(F32)
    for k, send_ref in enumerate(send_refs):
        part = pl.ds(pl.multiple_of(jnp.bitwise_xor(mate_ref[0], k) * dim, 16), dim)
        send_ref[0:dim, :] = q_ref[0, part, :]
        send_ref[dim : 2 * dim, :] = k_ref[0, part, :]
        send_ref[2 * dim : 3 * dim, :] = v_ref[0, part, :]
        send_ref[3 * dim : 4 * dim, :] = (g_ref[0, part, :].astype(F32) * weight).astype(BF16)


def unpack_kernel(mates, dim, mate_ref, *refs):
    for k in range(mates):
        part = pl.ds(pl.multiple_of(jnp.bitwise_xor(mate_ref[0], k) * dim, 16), dim)
        for n, out_ref in enumerate(refs[mates:]):
            out_ref[0, part, :] = refs[k][n * dim : (n + 1) * dim, :]


def copies_in(far_ref, near_ref, sems, block):
    return [
        pltpu.make_async_copy(far_ref.at[:, pl.ds(p, block)], near_ref.at[:, pl.ds(p, block)], sems.at[n])
        for n, p in enumerate(range(0, near_ref.shape[1], block))
    ]


def centred(pair):
    halves, block, cols, chan = pair.shape
    rows = pair.astype(F32).reshape(halves * block * cols, chan)
    return rows - jnp.mean(rows, axis=-1, keepdims=True)


def pieces(values, halves, block, cols):
    many = 2 if block % 2 == 0 else 1
    for p in range(0, block, many):
        starts = [(h * block + p + n) * cols for n in range(many) for h in range(halves)]
        yield p, many, jnp.concatenate([values[x : x + cols] for x in starts], axis=0)


def from_halves(block, cols):
    turned = block.T
    return jnp.concatenate([turned[:cols], turned[cols:]], axis=1)


def to_halves(block):
    half = block.shape[1] // 2
    return jnp.concatenate([block[:, :half], block[:, half:]], axis=0).T


def norm_kernel(groups, mates, block, far_ref, gain_ref, proj_ref, send_ref, pair_s, sems, bias_s):
    halves, half, cols, chan = pair_s.shape
    heads = proj_ref.shape[0]
    copies = copies_in(far_ref, pair_s, sems, block)
    for copy in copies:
        copy.start()
    for step, copy in enumerate(copies):
        copy.wait()
        cent = centred(pair_s[:, step * block : (step + 1) * block])
        inv_std = lax.rsqrt(jnp.mean(cent * cent, axis=-1, keepdims=True) + EPS)
        lnout = (cent * inv_std * gain_ref[...]).astype(BF16)
        for p, many, piece in pieces(lnout, halves, block, cols):
            bias = dot(proj_ref[...], piece, NT)
            for n in range(many):
                bias_s[pl.ds(step * block + p + n, heads, stride=half), :] = bias[
                    :, n * halves * cols : (n + 1) * halves * cols
                ]
    local = send_ref.shape[0] // (groups * mates)
    for h in range(heads):
        tile = from_halves(bias_s[h * half : (h + 1) * half, :], cols).astype(BF16)
        for g in range(groups):
            send_ref[(g * mates + h % mates) * local + h // mates] = tile


def prepare_kernel(block, far_ref, cent_ref, inv_ref, pair_s, cent_s, sems, out_sems, var_s):
    halves, half, cols, chan = pair_s.shape
    copies = copies_in(far_ref, pair_s, sems, block)
    outs = copies_in(cent_s, cent_ref, out_sems, block)
    for copy in copies:
        copy.start()
    ones = jnp.full((16, chan), 1.0, BF16)
    for step, copy in enumerate(copies):
        copy.wait()
        part = slice(step * block, (step + 1) * block)
        cent = centred(pair_s[:, part])
        cent_s[:, part] = cent.astype(BF16).reshape(halves, block, cols, chan)
        outs[step].start()
        for p, many, piece in pieces((cent * cent).astype(BF16), halves, block, cols):
            var = dot(ones, piece, NT)[:1] * (1.0 / chan)
            for n in range(many):
                var_s[pl.ds(step * block + p + n, 1), :] = var[:, n * halves * cols : (n + 1) * halves * cols]
    inv_ref[...] = lax.rsqrt(from_halves(var_s[...], cols) + EPS)
    for copy in outs:
        copy.wait()


def attend_kernel(samples, wide, *refs):
    got_refs, refs = refs[:samples], refs[samples:]
    bias_ref, mask_ref, refs = refs[0], refs[1], refs[2:]
    back_refs, refs = refs[:samples], refs[samples:]
    grad_ref, key_s, value_s, dk_s, dv_s = refs
    four, count = got_refs[0].shape
    dim = four // 4
    root = 1.0 / math.sqrt(dim)
    samp, heads, cols, rows = bias_ref.shape
    first = lax.broadcasted_iota(jnp.int32, (16, count), 0) == 0
    mask_rows = jnp.where(first & (mask_ref[...] <= 0), MASKED, 0.0).astype(BF16)
    one_rows = jnp.where(lax.broadcasted_iota(jnp.int32, (16, wide), 0) == 0, 1.0, 0.0).astype(BF16)
    for s in range(samples):
        keys = got_refs[s][dim : 2 * dim, :]
        key_s[s] = jnp.concatenate([keys, keys, mask_rows], axis=0).T
        value_s[s] = got_refs[s][2 * dim : 3 * dim, :].T
    per = wide // rows
    for a in range(count // wide):
        lanes = slice(a * wide, (a + 1) * wide)
        bias = jnp.concatenate(
            [bias_ref[:, a * per + p].reshape(count, rows) for p in range(per)], axis=1
        ).astype(F32) * LOG2E
        total = None
        for s in range(samples):
            query = got_refs[s][0:dim, lanes]
            scaled = query.astype(F32) * (LOG2E * root)
            upper = scaled.astype(BF16)
            lower = (scaled - upper.astype(F32)).astype(BF16)
            scores = dot(key_s[s], jnp.concatenate([upper, lower, one_rows], axis=0)) + bias
            expo = jnp.exp2(scores - jnp.max(scores, axis=0, keepdims=True))
            inv_sum = 1.0 / jnp.sum(expo, axis=0, keepdims=True)
            expo_b = expo.astype(BF16)
            out = dot(got_refs[s][2 * dim : 3 * dim, :], expo_b) * inv_sum
            back_refs[s][0:dim, lanes] = out.astype(BF16)
            grad = (got_refs[s][3 * dim : 4 * dim, lanes].astype(F32) * inv_sum).astype(BF16)
            row_dot = jnp.sum(grad.astype(F32) * out, axis=0, keepdims=True)
            dscore = expo * (dot(value_s[s], grad) - row_dot)
            total = dscore if total is None else total + dscore
            dscore_b = dscore.astype(BF16)
            back_refs[s][dim : 2 * dim, lanes] = (
                dot(got_refs[s][dim : 2 * dim, :], dscore_b) * root
            ).astype(BF16)
            dk = dot(query, dscore_b, NT)
            dv = dot(grad, expo_b, NT)
            if a == 0:
                dk_s[s] = dk
                dv_s[s] = dv
            else:
                dk_s[s] += dk
                dv_s[s] += dv
        total = total.astype(BF16)
        for p in range(per):
            grad_ref[:, a * per + p] = total[:, p * rows : (p + 1) * rows].reshape(samp, cols, rows)
    for s in range(samples):
        back_refs[s][2 * dim : 3 * dim, :] = (dk_s[s] * root).astype(BF16)
        back_refs[s][3 * dim : 4 * dim, :] = dv_s[s].astype(BF16)


def reduce_kernel(groups, mates, block, got_ref, inv_ref, far_ref, sum_ref, cent_s, sems, plain_s):
    halves, half, cols, chan = cent_s.shape
    devices, heads, _ = sum_ref.shape
    copies = copies_in(far_ref, cent_s, sems, block)
    for copy in copies:
        copy.start()
    for h in range(heads):
        plain = gathered(groups, mates, heads, h, got_ref) * inv_ref[...]
        plain_s[h * half : (h + 1) * half, :] = to_halves(plain)
    total = jnp.zeros((heads, chan), F32)
    for step, copy in enumerate(copies):
        copy.wait()
        for p in range(step * block, (step + 1) * block):
            plain = plain_s[pl.ds(p, heads, stride=half), :].astype(BF16)
            total += dot(plain, jnp.concatenate([cent_s[h, p] for h in range(halves)], axis=0))
    rounded = total.astype(BF16)
    for n in range(devices):
        sum_ref[n] = rounded


def place(mates, heads, h):
    return (h % mates) * (heads // mates) + h // mates


def gathered(groups, mates, heads, h, got_ref):
    at = place(mates, heads, h)
    grad = got_ref[at].astype(F32)
    for g in range(1, groups):
        grad += got_ref[g * heads + at].astype(F32)
    return grad


def pair_kernel(
    groups, mates, block, got_ref, bias_ref, inv_ref, gain_ref, proj_ref, far_ref, out_ref,
    cent_s, out_s, sems, out_sems, plain_s, biased_s,
):
    halves, half, cols, chan = cent_s.shape
    heads = proj_ref.shape[0]
    copies = copies_in(far_ref, cent_s, sems, block)
    outs = copies_in(out_s, out_ref, out_sems, block)
    for copy in copies:
        copy.start()
    scaled = proj_ref[...].astype(F32) * gain_ref[...]
    scaled = (scaled - jnp.mean(scaled, axis=1, keepdims=True)).astype(BF16)
    none = jnp.zeros((heads, chan), BF16)
    ones = jnp.ones((heads, chan), BF16)
    right = jnp.concatenate(
        [jnp.concatenate([scaled, none], axis=1), jnp.concatenate([none, ones], axis=1)], axis=0
    )
    inv_std = inv_ref[...]
    for h in range(heads):
        plain = gathered(groups, mates, heads, h, got_ref) * inv_std
        biased = plain * inv_std * bias_ref[place(mates, heads, h)].astype(F32) * (1.0 / chan)
        plain_s[h * half : (h + 1) * half, :] = to_halves(plain)
        biased_s[h * half : (h + 1) * half, :] = to_halves(biased)
    for step, copy in enumerate(copies):
        copy.wait()
        for p in range(step * block, (step + 1) * block):
            take = pl.ds(p, heads, stride=half)
            left = jnp.concatenate([plain_s[take, :], biased_s[take, :]], axis=0).astype(BF16)
            both = dot(left, right, TN)
            for h in range(halves):
                part = slice(h * cols, (h + 1) * cols)
                out_s[h, p] = (both[part, :chan] - cent_s[h, p].astype(F32) * both[part, chan:]).astype(BF16)
        outs[step].start()
    for copy in outs:
        copy.wait()


def final_kernel(scale, sums_ref, gain_ref, proj_ref, weight_ref, gain_grad_ref):
    total = sums_ref[0].astype(F32)
    for n in range(1, sums_ref.shape[0]):
        total += sums_ref[n].astype(F32)
    total = total * scale
    weight_ref[...] = total * gain_ref[...]
    gain_grad_ref[...] = jnp.sum(total * proj_ref[...].astype(F32), axis=0, keepdims=True)


def local(groups, mates, axes, queries, keys, values, out_grad, pair, ln_gain, proj_weight, token_mask, atom_map):
    _, width, count = queries.shape
    rows, cols, chan = pair.shape
    heads = proj_weight.shape[1]
    dim = width // mates
    head_parts = heads // mates
    devices = groups * mates * head_parts
    entries = rows * cols
    half = rows // 2
    gain_row = ln_gain.reshape(1, chan)
    proj_rows = proj_weight.T
    mask_row = token_mask.reshape(1, count)
    pair = pair.reshape(2, half, cols, chan)
    mate = lax.axis_index(axes[1]).astype(jnp.int32).reshape(1)
    whole = lambda *shape: pl.BlockSpec(shape, lambda *_: (0,) * len(shape))
    scalar = pl.BlockSpec(memory_space=pltpu.SMEM)
    vector = pl.BlockSpec(memory_space=pltpu.VMEM)

    def swap(chunks):
        return [
            lax.ppermute(x, axes[1], [(i, i ^ k) for i in range(mates)]) if k else x
            for k, x in enumerate(chunks)
        ]

    block = step_of(half, 16)
    far = pl.BlockSpec(memory_space=pltpu.HBM)
    tiles = jax.ShapeDtypeStruct((devices, cols, rows), BF16)
    by_head = pltpu.VMEM((heads * half, 2 * cols), F32)
    near = pltpu.VMEM(pair.shape, BF16)
    sems = pltpu.SemaphoreType.DMA((half // block,))

    bias_send = call(
        functools.partial(norm_kernel, groups, mates, block), "norm", 2 * entries * chan * heads,
        2 * entries * chan, BIG,
        out_shape=tiles,
        in_specs=[far, vector, vector],
        out_specs=vector,
        scratch_shapes=[near, sems, by_head],
    )(pair, gain_row, proj_rows)
    bias = lax.all_to_all(bias_send, axes, 0, 0, tiled=True)

    chunks = (jax.ShapeDtypeStruct((4 * dim, count), BF16),) * mates
    send = call(
        functools.partial(pack_kernel, dim), "pack", 2 * 16 * 128 * atom_map.shape[0],
        16 * width * count, BIG, out_shape=chunks, in_specs=[scalar] + [vector] * 6,
    )(mate, queries, keys, values, out_grad, atom_map.reshape(1, -1), mask_row)
    got = swap(send)

    cent, inv_std = call(
        functools.partial(prepare_kernel, block), "prepare", 2 * entries * chan * heads, 4 * entries * chan, BIG,
        out_shape=(
            jax.ShapeDtypeStruct(pair.shape, BF16),
            jax.ShapeDtypeStruct((cols, rows), F32),
        ),
        in_specs=[far],
        out_specs=(far, vector),
        scratch_shapes=[near, near, sems, sems, pltpu.VMEM((half, 2 * cols), F32)],
    )(pair)

    fine = rows % 128 == 0
    samp = groups * mates
    bias = bias.reshape(samp, head_parts, cols, rows)
    if not fine:
        bias = bias.transpose(0, 2, 1, 3).reshape(1, 1, count, count)
    wide = max(rows, step_of(count, 256)) if fine else count
    *back, grads = call(
        functools.partial(attend_kernel, mates, wide), "attend", 12 * mates * dim * count * count,
        8 * mates * dim * count * 2 + 4 * count * count, BIG,
        out_shape=chunks + (jax.ShapeDtypeStruct(bias.shape, BF16),),
        scratch_shapes=[
            pltpu.VMEM((mates, count, 2 * dim + 16), BF16),
            pltpu.VMEM((mates, count, dim), BF16),
            pltpu.VMEM((mates, dim, count), F32),
            pltpu.VMEM((mates, dim, count), F32),
        ],
    )(*got, bias, mask_row)
    if not fine:
        grads = grads.reshape(samp, cols, head_parts, rows).transpose(0, 2, 1, 3)
    grads = lax.all_to_all(grads.reshape(devices, cols, rows), axes, 0, 0, tiled=True)
    swapped = swap(back)
    parts = call(
        functools.partial(reduce_kernel, groups, mates, block), "reduce", 2 * entries * chan * heads,
        2 * entries * chan, BIG,
        out_shape=jax.ShapeDtypeStruct((devices, heads, chan), BF16),
        in_specs=[vector, vector, far],
        out_specs=vector,
        scratch_shapes=[near, sems, by_head],
    )(grads, inv_std, cent)
    sums = lax.all_to_all(parts, axes, 0, 0, tiled=True)

    pair_grad = call(
        functools.partial(pair_kernel, groups, mates, block), "pair_grad", 8 * entries * chan * heads,
        4 * entries * chan, BIG,
        out_shape=jax.ShapeDtypeStruct(pair.shape, BF16),
        in_specs=[vector] * 5 + [far],
        out_specs=far,
        scratch_shapes=[near, near, sems, sems, by_head, by_head],
    )(grads, bias_send, inv_std, gain_row, proj_rows, cent)
    pair_grad, swapped = lax.optimization_barrier((pair_grad, swapped))
    attended, query_grad, key_grad, value_grad = call(
        functools.partial(unpack_kernel, mates, dim), "unpack", 0, 16 * width * count, BIG,
        out_shape=(jax.ShapeDtypeStruct(queries.shape, BF16),) * 4,
        in_specs=[scalar] + [vector] * mates,
    )(mate, *swapped)
    weight_rows, gain_grad = call(
        functools.partial(final_kernel, 1.0 / count), "final", 0, 2 * devices * heads * chan, BIG,
        out_shape=(
            jax.ShapeDtypeStruct((heads, chan), F32),
            jax.ShapeDtypeStruct((1, chan), F32),
        ),
    )(sums, gain_row, proj_rows)
    return (
        attended, query_grad, key_grad, value_grad,
        pair_grad.reshape(rows, cols, chan), weight_rows.T, gain_grad.reshape(chan),
    )


def solution(mesh):
    samp, head = mesh.axis_names
    samp_size, head_size = mesh.shape[samp], mesh.shape[head]

    def run(*args):
        heads = args[6].shape[1]
        mates = math.gcd(heads // head_size, samp_size)
        groups = samp_size // mates
        axes = ("group", "mate", "part")
        fine = Mesh(mesh.devices.reshape(groups, mates, head_size), axes)
        by_sample = P(("group", "mate"), "part", None)
        by_pair = P("part", ("group", "mate"), None)
        return jax.shard_map(
            functools.partial(local, groups, mates, axes),
            mesh=fine,
            in_specs=(by_sample,) * 4 + (by_pair,) + (P(),) * 4,
            out_specs=(by_sample,) * 4 + (by_pair, P(), P()),
            check_vma=False,
        )(*args)

    return run
```

```python
import functools
import math

import jax
import jax.numpy as jnp
from jax import lax
from jax.experimental import pallas as pl
from jax.experimental.pallas import tpu as pltpu
from jax.sharding import Mesh
from jax.sharding import PartitionSpec as P

F32 = jnp.float32
BF16 = jnp.bfloat16
LOG2E = math.log2(math.e)
EPS = 1e-05
MASKED = -1000000000.0
BIG = 60
SMALL = 24
SPLIT = 1
ORDER = (0, 2, 1, 3)
FIRST = (2,)
EARLY = (1, 3)
NT = (((1,), (1,)), ((), ()))
TN = (((0,), (0,)), ((), ()))


def dot(a, b, dims=(((1,), (0,)), ((), ()))):
    return lax.dot_general(a, b, dims, preferred_element_type=F32)


def call(kernel, name, flops, moved, mebi, **kw):
    return pl.pallas_call(
        kernel,
        name=name,
        compiler_params=pltpu.CompilerParams(vmem_limit_bytes=mebi * 1024 * 1024),
        cost_estimate=pl.CostEstimate(flops=flops, bytes_accessed=moved, transcendentals=0),
        **kw,
    )


def together(value, chunks, some):
    some = [k for k in some if k < len(chunks)]
    if not some:
        return value, chunks
    value, taken = lax.optimization_barrier((value, [chunks[k] for k in some]))
    return value, [taken[some.index(k)] if k in some else x for k, x in enumerate(chunks)]


def step_of(count, most):
    return max(n for n in range(1, most + 1) if count % n == 0)


def pack_kernel(dim, mate_ref, q_ref, k_ref, v_ref, g_ref, map_ref, mask_ref, *refs):
    *send_refs, grad_s, sems = refs
    copies = []
    for k, send_ref in enumerate(send_refs):
        part = pl.ds(pl.multiple_of(jnp.bitwise_xor(mate_ref[0], k) * dim, 16), dim)
        for n, from_ref in enumerate((q_ref, k_ref, v_ref, g_ref)):
            to_ref = grad_s.at[k] if n == 3 else send_ref.at[n * dim : (n + 1) * dim]
            copies.append(pltpu.make_async_copy(from_ref.at[0, part], to_ref, sems.at[k, n]))
    for copy in copies:
        copy.start()
    count = mask_ref.shape[1]
    atoms = map_ref.shape[1]
    rows = pl.cdiv(count, 128)
    tall = pl.cdiv(rows, 16) * 16
    token = map_ref[...]
    high = lax.shift_right_logical(token, 7)
    low = jnp.bitwise_and(token, 127)
    is_row = (lax.broadcasted_iota(jnp.int32, (tall, atoms), 0) == high).astype(F32).astype(BF16)
    is_lane = (lax.broadcasted_iota(jnp.int32, (128, atoms), 0) == low).astype(F32).astype(BF16)
    counts = dot(is_row, is_lane, NT)
    line = jnp.concatenate([counts[r : r + 1, :] for r in range(rows)], axis=1)[:, :count]
    weight = line * (count / atoms) * mask_ref[...].astype(F32)
    for copy in copies:
        copy.wait()
    for k, send_ref in enumerate(send_refs):
        send_ref[3 * dim : 4 * dim, :] = (grad_s[k].astype(F32) * weight).astype(BF16)


def unpack_kernel(mates, dim, mate_ref, *refs):
    for k in range(mates):
        part = pl.ds(pl.multiple_of(jnp.bitwise_xor(mate_ref[0], k) * dim, 16), dim)
        for n, out_ref in enumerate(refs[mates:]):
            out_ref[0, part, :] = refs[k][n * dim : (n + 1) * dim, :]


def copies_of(near_ref, far_ref, sems, block):
    return [
        pltpu.make_async_copy(near_ref.at[:, pl.ds(p, block)], far_ref.at[:, pl.ds(p, block)], sems.at[n])
        for n, p in enumerate(range(0, near_ref.shape[1], block))
    ]


def centred(pair):
    halves, block, cols, chan = pair.shape
    rows = pair.reshape(halves * block * cols, chan)
    return rows.astype(F32) - dot(rows, jnp.full((chan, chan), 1.0, BF16)) * (1.0 / chan)


def pieces(values, halves, block, cols):
    many = 2 if block % 2 == 0 else 1
    for p in range(0, block, many):
        starts = [(h * block + p + n) * cols for n in range(many) for h in range(halves)]
        yield p, many, jnp.concatenate([values[x : x + cols] for x in starts], axis=0)


def from_halves(block, cols):
    turned = block.T
    return jnp.concatenate([turned[:cols], turned[cols:]], axis=1)


def to_halves(block):
    half = block.shape[1] // 2
    return jnp.concatenate([block[:, :half], block[:, half:]], axis=0).T


def norm_kernel(groups, mates, block, pair_ref, gain_ref, proj_ref, send_ref, bias_s):
    halves, half, cols, chan = pair_ref.shape
    heads = proj_ref.shape[0]
    for first in range(0, half, block):
        cent = centred(pair_ref[:, first : first + block])
        inv_std = lax.rsqrt(jnp.mean(cent * cent, axis=-1, keepdims=True) + EPS)
        lnout = (cent * inv_std * gain_ref[...]).astype(BF16)
        for p, many, piece in pieces(lnout, halves, block, cols):
            bias = dot(proj_ref[...], piece, NT)
            for n in range(many):
                bias_s[pl.ds(first + p + n, heads, stride=half), :] = bias[
                    :, n * halves * cols : (n + 1) * halves * cols
                ]
    pairs = 2 if heads % 2 == 0 else 1
    for h in range(0, heads, pairs):
        turned = bias_s[h * half : (h + pairs) * half, :].T.astype(BF16)
        for n in range(pairs):
            part = slice(n * half, (n + 1) * half)
            tile = jnp.concatenate([turned[:cols, part], turned[cols:, part]], axis=1)
            for g in range(groups):
                send_ref[g * heads + place(mates, heads, h + n)] = tile


def prepare_kernel(block, pair_ref, inv_ref, var_s):
    halves, half, cols, chan = pair_ref.shape
    ones = jnp.full((16, chan), 1.0, BF16)
    for start in range(0, half, block):
        part = slice(start, start + block)
        cent = centred(pair_ref[:, part])
        for p, many, piece in pieces((cent * cent).astype(BF16), halves, block, cols):
            var = dot(ones, piece, NT)[:1] * (1.0 / chan)
            for n in range(many):
                var_s[pl.ds(start + p + n, 1), :] = var[:, n * halves * cols : (n + 1) * halves * cols]
    inv_ref[...] = lax.rsqrt(from_halves(var_s[...], cols) + EPS)


def attend_kernel(samples, wide, last, *refs):
    got_refs, refs = refs[:samples], refs[samples:]
    bias_ref, mask_ref, refs = refs[0], refs[1], refs[2:]
    before_ref, refs = (None, refs) if len(refs) == samples + 5 else (refs[0], refs[1:])
    back_refs, refs = refs[:samples], refs[samples:]
    grad_ref, key_s, value_s, dk_s, dv_s = refs
    four, count = got_refs[0].shape
    dim = four // 4
    root = 1.0 / math.sqrt(dim)
    samp, heads, cols, rows = bias_ref.shape
    first = lax.broadcasted_iota(jnp.int32, (16, count), 0) == 0
    mask_rows = jnp.where(first & (mask_ref[...] <= 0), MASKED, 0.0).astype(BF16)
    one_rows = jnp.where(lax.broadcasted_iota(jnp.int32, (16, wide), 0) == 0, 1.0, 0.0).astype(BF16)
    for s, got_ref in enumerate(got_refs):
        keys = got_ref[dim : 2 * dim, :]
        key_s[s] = jnp.concatenate([keys, keys, mask_rows], axis=0).T
        value_s[s] = got_ref[2 * dim : 3 * dim, :].T
    per = wide // rows
    for a in range(count // wide):
        lanes = slice(a * wide, (a + 1) * wide)
        bias = jnp.concatenate(
            [bias_ref[:, a * per + p].reshape(count, rows) for p in range(per)], axis=1
        ).astype(F32) * LOG2E
        total = None if before_ref is None else before_ref[:, lanes]
        for s, (got_ref, back_ref) in enumerate(zip(got_refs, back_refs)):
            query = got_ref[0:dim, lanes]
            scaled = query.astype(F32) * (LOG2E * root)
            upper = scaled.astype(BF16)
            lower = (scaled - upper.astype(F32)).astype(BF16)
            scores = dot(key_s[s], jnp.concatenate([upper, lower, one_rows], axis=0)) + bias
            expo = jnp.exp2(scores - jnp.max(scores, axis=0, keepdims=True))
            inv_sum = 1.0 / jnp.sum(expo, axis=0, keepdims=True)
            expo_b = expo.astype(BF16)
            out = dot(got_ref[2 * dim : 3 * dim, :], expo_b) * inv_sum
            back_ref[0:dim, lanes] = out.astype(BF16)
            grad = (got_ref[3 * dim : 4 * dim, lanes].astype(F32) * inv_sum).astype(BF16)
            row_dot = jnp.sum(grad.astype(F32) * out, axis=0, keepdims=True)
            dscore = expo * (dot(value_s[s], grad) - row_dot)
            total = dscore if total is None else total + dscore
            dscore_b = dscore.astype(BF16)
            back_ref[dim : 2 * dim, lanes] = (dot(got_ref[dim : 2 * dim, :], dscore_b) * root).astype(BF16)
            dk = dot(query, dscore_b, NT)
            dv = dot(grad, expo_b, NT)
            if a == 0:
                dk_s[s] = dk
                dv_s[s] = dv
            else:
                dk_s[s] += dk
                dv_s[s] += dv
        if not last:
            grad_ref[:, lanes] = total
            continue
        total = total.astype(BF16)
        for p in range(per):
            grad_ref[:, a * per + p] = total[:, p * rows : (p + 1) * rows].reshape(samp, cols, rows)
    for s, back_ref in enumerate(back_refs):
        back_ref[2 * dim : 3 * dim, :] = (dk_s[s] * root).astype(BF16)
        back_ref[3 * dim : 4 * dim, :] = dv_s[s].astype(BF16)


def reduce_kernel(groups, mates, got_ref, inv_ref, pair_ref, sum_ref, plain_s):
    halves, half, cols, chan = pair_ref.shape
    devices, heads, _ = sum_ref.shape
    for h in range(heads):
        plain = gathered(groups, mates, heads, h, got_ref) * inv_ref[...]
        plain_s[h * half : (h + 1) * half, :] = to_halves(plain)
    total = jnp.zeros((heads, chan), F32)
    for p in range(half):
        plain = plain_s[pl.ds(p, heads, stride=half), :].astype(BF16)
        total += dot(plain, jnp.concatenate([pair_ref[h, p] for h in range(halves)], axis=0))
    total = (total - jnp.mean(total, axis=1, keepdims=True)).astype(BF16)
    for n in range(devices):
        sum_ref[n] = total


def place(mates, heads, h):
    return (h % mates) * (heads // mates) + h // mates


def gathered(groups, mates, heads, h, got_ref):
    at = place(mates, heads, h)
    grad = got_ref[at].astype(F32)
    for g in range(1, groups):
        grad += got_ref[g * heads + at].astype(F32)
    return grad


def pair_kernel(
    groups, mates, block, got_ref, bias_ref, inv_ref, gain_ref, proj_ref, pair_ref, out_ref,
    out_s, sems, plain_s, biased_s,
):
    halves, half, cols, chan = pair_ref.shape
    heads = proj_ref.shape[0]
    outs = copies_of(out_s, out_ref, sems, block)
    scaled = proj_ref[...].astype(F32) * gain_ref[...]
    scaled = (scaled - jnp.mean(scaled, axis=1, keepdims=True)).astype(BF16)
    none = jnp.zeros((heads, chan), BF16)
    ones = jnp.ones((heads, chan), BF16)
    right = jnp.concatenate(
        [jnp.concatenate([scaled, none], axis=1), jnp.concatenate([none, ones], axis=1)], axis=0
    )
    inv_std = inv_ref[...]
    for h in range(heads):
        plain = gathered(groups, mates, heads, h, got_ref) * inv_std
        biased = plain * inv_std * bias_ref[place(mates, heads, h)].astype(F32) * (1.0 / chan)
        plain_s[h * half : (h + 1) * half, :] = to_halves(plain)
        biased_s[h * half : (h + 1) * half, :] = to_halves(biased)
    for step, copy in enumerate(outs):
        first = step * block
        cent = centred(pair_ref[:, first : first + block]).reshape(halves, block, cols, chan)
        for p in range(first, first + block):
            take = pl.ds(p, heads, stride=half)
            left = jnp.concatenate([plain_s[take, :], biased_s[take, :]], axis=0).astype(BF16)
            both = dot(left, right, TN)
            for h in range(halves):
                part = slice(h * cols, (h + 1) * cols)
                out_s[h, p] = (both[part, :chan] - cent[h, p - first] * both[part, chan:]).astype(BF16)
        copy.start()
    for copy in outs:
        copy.wait()


def final_kernel(scale, sums_ref, gain_ref, proj_ref, weight_ref, gain_grad_ref):
    total = sums_ref[0].astype(F32)
    for n in range(1, sums_ref.shape[0]):
        total += sums_ref[n].astype(F32)
    total = total * scale
    weight_ref[...] = total * gain_ref[...]
    gain_grad_ref[...] = jnp.sum(total * proj_ref[...].astype(F32), axis=0, keepdims=True)


def local(groups, mates, axes, queries, keys, values, out_grad, pair, ln_gain, proj_weight, token_mask, atom_map):
    _, width, count = queries.shape
    rows, cols, chan = pair.shape
    heads = proj_weight.shape[1]
    dim = width // mates
    head_parts = heads // mates
    devices = groups * mates * head_parts
    entries = rows * cols
    half = rows // 2
    gain_row = ln_gain.reshape(1, chan)
    proj_rows = proj_weight.T
    mask_row = token_mask.reshape(1, count)
    pair = pair.reshape(2, half, cols, chan)
    mate = lax.axis_index(axes[1]).astype(jnp.int32).reshape(1)
    whole = lambda *shape: pl.BlockSpec(shape, lambda *_: (0,) * len(shape))
    scalar = pl.BlockSpec(memory_space=pltpu.SMEM)
    vector = pl.BlockSpec(memory_space=pltpu.VMEM)

    def swap(chunks):
        return [
            lax.ppermute(x, axes[1], [(i, i ^ k) for i in range(mates)]) if k else x
            for k, x in enumerate(chunks)
        ]

    block = step_of(half, 16)
    far = pl.BlockSpec(memory_space=pltpu.HBM)
    tiles = jax.ShapeDtypeStruct((devices, cols, rows), BF16)
    by_head = pltpu.VMEM((heads * half, 2 * cols), F32)
    near = pltpu.VMEM(pair.shape, BF16)
    sems = pltpu.SemaphoreType.DMA((half // block,))

    chunks = (jax.ShapeDtypeStruct((4 * dim, count), BF16),) * mates
    send = call(
        functools.partial(pack_kernel, dim), "pack", 2 * 16 * 128 * atom_map.shape[0],
        16 * width * count, SMALL, out_shape=chunks,
        in_specs=[scalar] + [far] * 4 + [vector] * 2,
        out_specs=(vector,) * mates,
        scratch_shapes=[pltpu.VMEM((mates, dim, count), BF16), pltpu.SemaphoreType.DMA((mates, 4))],
    )(mate, queries, keys, values, out_grad, atom_map.reshape(1, -1), mask_row)
    got = swap(send)

    bias_send = call(
        functools.partial(norm_kernel, groups, mates, block), "norm", 2 * entries * chan * heads,
        2 * entries * chan, BIG,
        out_shape=tiles,
        in_specs=[vector] * 3,
        out_specs=vector,
        scratch_shapes=[by_head],
    )(pair, gain_row, proj_rows)
    bias = lax.all_to_all(bias_send, axes, 0, 0, tiled=True)

    inv_std = call(
        functools.partial(prepare_kernel, block), "prepare", 2 * entries * chan * heads, 2 * entries * chan, SMALL,
        out_shape=jax.ShapeDtypeStruct((cols, rows), F32),
        in_specs=[vector],
        out_specs=vector,
        scratch_shapes=[pltpu.VMEM((half, 2 * cols), F32)],
    )(pair)

    fine = rows % 128 == 0
    samp = groups * mates
    bias = bias.reshape(samp, head_parts, cols, rows)
    if not fine:
        bias = bias.transpose(0, 2, 1, 3).reshape(1, 1, count, count)
    wide = max(rows, step_of(count, 256)) if fine else count
    order = sorted(range(mates), key=lambda k: ORDER.index(k) if k in ORDER else k)
    back, before = [None] * mates, ()
    for n in range(0, mates, SPLIT):
        part = order[n : n + SPLIT]
        many, last = len(part), n + SPLIT >= mates
        *outs, grads = call(
            functools.partial(attend_kernel, many, wide, last), "attend", 12 * many * dim * count * count,
            8 * many * dim * count * 2 + 4 * count * count, SMALL,
            out_shape=chunks[:many]
            + (jax.ShapeDtypeStruct(bias.shape, BF16) if last else jax.ShapeDtypeStruct((count, count), F32),),
            scratch_shapes=[
                pltpu.VMEM((many, count, 2 * dim + 16), BF16),
                pltpu.VMEM((many, count, dim), BF16),
                pltpu.VMEM((many, dim, count), F32),
                pltpu.VMEM((many, dim, count), F32),
            ],
        )(*[got[k] for k in part], bias, mask_row, *before)
        before = (grads,)
        for k, x in zip(part, outs):
            back[k] = x
    if not fine:
        grads = grads.reshape(samp, cols, head_parts, rows).transpose(0, 2, 1, 3)
    swapped = swap(back)
    grads, swapped = together(grads, swapped, FIRST)
    grads = lax.all_to_all(grads.reshape(devices, cols, rows), axes, 0, 0, tiled=True)
    parts = call(
        functools.partial(reduce_kernel, groups, mates), "reduce", 2 * entries * chan * heads,
        2 * entries * chan, SMALL,
        out_shape=jax.ShapeDtypeStruct((devices, heads, chan), BF16),
        in_specs=[vector] * 3,
        out_specs=vector,
        scratch_shapes=[by_head],
    )(grads, inv_std, pair)
    parts, swapped = together(parts, swapped, EARLY)
    sums = lax.all_to_all(parts, axes, 0, 0, tiled=True)

    pair_grad = call(
        functools.partial(pair_kernel, groups, mates, block), "pair_grad", 8 * entries * chan * heads,
        4 * entries * chan, SMALL,
        out_shape=jax.ShapeDtypeStruct(pair.shape, BF16),
        in_specs=[vector] * 6,
        out_specs=far,
        scratch_shapes=[near, sems, by_head, by_head],
    )(grads, bias_send, inv_std, gain_row, proj_rows, pair)
    pair_grad, swapped = lax.optimization_barrier((pair_grad, swapped))
    attended, query_grad, key_grad, value_grad = call(
        functools.partial(unpack_kernel, mates, dim), "unpack", 0, 16 * width * count, SMALL,
        out_shape=(jax.ShapeDtypeStruct(queries.shape, BF16),) * 4,
        in_specs=[scalar] + [vector] * mates,
    )(mate, *swapped)
    weight_rows, gain_grad = call(
        functools.partial(final_kernel, 1.0 / count), "final", 0, 2 * devices * heads * chan, SMALL,
        out_shape=(
            jax.ShapeDtypeStruct((heads, chan), F32),
            jax.ShapeDtypeStruct((1, chan), F32),
        ),
    )(sums, gain_row, proj_rows)
    return (
        attended, query_grad, key_grad, value_grad,
        pair_grad.reshape(rows, cols, chan), weight_rows.T, gain_grad.reshape(chan),
    )


def solution(mesh):
    samp, head = mesh.axis_names
    samp_size, head_size = mesh.shape[samp], mesh.shape[head]

    def run(*args):
        heads = args[6].shape[1]
        mates = math.gcd(heads // head_size, samp_size)
        groups = samp_size // mates
        axes = ("group", "mate", "part")
        fine = Mesh(mesh.devices.reshape(groups, mates, head_size), axes)
        by_sample = P(("group", "mate"), "part", None)
        by_pair = P("part", ("group", "mate"), None)
        return jax.shard_map(
            functools.partial(local, groups, mates, axes),
            mesh=fine,
            in_specs=(by_sample,) * 4 + (by_pair,) + (P(),) * 4,
            out_specs=(by_sample,) * 4 + (by_pair, P(), P()),
            check_vma=False,
        )(*args)

    return run
```

```python
import functools
import math

import jax
import jax.numpy as jnp
from jax import lax
from jax.experimental import pallas as pl
from jax.experimental.pallas import tpu as pltpu
from jax.sharding import Mesh
from jax.sharding import PartitionSpec as P

F32 = jnp.float32
BF16 = jnp.bfloat16
LOG2E = math.log2(math.e)
EPS = 1e-05
MASKED = -1000000000.0
BIG = 60
SMALL = 24
SPLIT = 1
ORDER = (0, 1, 2, 3)
FIRST = ()
NEXT = ()
EARLY = (3,)
LATE = (1, 2)
NT = (((1,), (1,)), ((), ()))
TN = (((0,), (0,)), ((), ()))


def dot(a, b, dims=(((1,), (0,)), ((), ()))):
    return lax.dot_general(a, b, dims, preferred_element_type=F32)


def call(kernel, name, flops, moved, mebi, **kw):
    return pl.pallas_call(
        kernel,
        name=name,
        compiler_params=pltpu.CompilerParams(vmem_limit_bytes=mebi * 1024 * 1024),
        cost_estimate=pl.CostEstimate(flops=flops, bytes_accessed=moved, transcendentals=0),
        **kw,
    )


def together(value, chunks, some):
    some = [k for k in some if k < len(chunks)]
    if not some:
        return value, chunks
    value, taken = lax.optimization_barrier((value, [chunks[k] for k in some]))
    return value, [taken[some.index(k)] if k in some else x for k, x in enumerate(chunks)]


def step_of(count, most):
    return max(n for n in range(1, most + 1) if count % n == 0)


def head_part(mate_ref, k, dim):
    return pl.ds(pl.multiple_of(jnp.bitwise_xor(mate_ref[0], k) * dim, 16), dim)


def pack_kernel(dim, mate_ref, *refs):
    from_refs, send_refs, sems = refs[:4], refs[4:-1], refs[-1]
    copies = [
        pltpu.make_async_copy(
            from_ref.at[0, head_part(mate_ref, k, dim)], send_ref.at[n * dim : (n + 1) * dim], sems.at[k, n]
        )
        for k, send_ref in enumerate(send_refs)
        for n, from_ref in enumerate(from_refs)
    ]
    for copy in copies:
        copy.start()
    for copy in copies:
        copy.wait()


def unpack_kernel(some, dim, mate_ref, *refs):
    *refs, sems = refs
    copies = [
        pltpu.make_async_copy(
            got_ref.at[n * dim : (n + 1) * dim], out_ref.at[0, head_part(mate_ref, k, dim)], sems.at[m, n]
        )
        for m, (k, got_ref) in enumerate(zip(some, refs))
        for n, out_ref in enumerate(refs[-4:])
    ]
    for copy in copies:
        copy.start()
    for copy in copies:
        copy.wait()


def weight_kernel(map_ref, mask_ref, weight_ref):
    count = mask_ref.shape[1]
    atoms = map_ref.shape[1]
    rows = pl.cdiv(count, 128)
    tall = pl.cdiv(rows, 16) * 16
    token = map_ref[...]
    high = lax.shift_right_logical(token, 7)
    low = jnp.bitwise_and(token, 127)
    is_row = (lax.broadcasted_iota(jnp.int32, (tall, atoms), 0) == high).astype(F32).astype(BF16)
    is_lane = (lax.broadcasted_iota(jnp.int32, (128, atoms), 0) == low).astype(F32).astype(BF16)
    counts = dot(is_row, is_lane, NT)
    line = jnp.concatenate([counts[r : r + 1, :] for r in range(rows)], axis=1)[:, :count]
    weight_ref[...] = line * (count / atoms) * mask_ref[...].astype(F32)


def copies_of(near_ref, far_ref, sems, block):
    return [
        pltpu.make_async_copy(near_ref.at[:, pl.ds(p, block)], far_ref.at[:, pl.ds(p, block)], sems.at[n])
        for n, p in enumerate(range(0, near_ref.shape[1], block))
    ]


def centred(pair):
    halves, block, cols, chan = pair.shape
    rows = pair.reshape(halves * block * cols, chan)
    return rows.astype(F32) - dot(rows, jnp.full((chan, chan), 1.0, BF16)) * (1.0 / chan)


def pieces(values, halves, block, cols):
    many = 2 if block % 2 == 0 else 1
    for p in range(0, block, many):
        starts = [(h * block + p + n) * cols for n in range(many) for h in range(halves)]
        yield p, many, jnp.concatenate([values[x : x + cols] for x in starts], axis=0)


def from_halves(block, cols):
    turned = block.T
    return jnp.concatenate([turned[:cols], turned[cols:]], axis=1)


def to_halves(block):
    half = block.shape[1] // 2
    return jnp.concatenate([block[:, :half], block[:, half:]], axis=0).T


def norm_kernel(groups, mates, block, pair_ref, gain_ref, proj_ref, send_ref, bias_s):
    halves, half, cols, chan = pair_ref.shape
    heads = proj_ref.shape[0]
    for first in range(0, half, block):
        cent = centred(pair_ref[:, first : first + block])
        inv_std = lax.rsqrt(jnp.mean(cent * cent, axis=-1, keepdims=True) + EPS)
        lnout = (cent * inv_std * gain_ref[...]).astype(BF16)
        for p, many, piece in pieces(lnout, halves, block, cols):
            bias = dot(proj_ref[...], piece, NT)
            for n in range(many):
                bias_s[pl.ds(first + p + n, heads, stride=half), :] = bias[
                    :, n * halves * cols : (n + 1) * halves * cols
                ]
    pairs = 2 if heads % 2 == 0 else 1
    for h in range(0, heads, pairs):
        turned = bias_s[h * half : (h + pairs) * half, :].T.astype(BF16)
        for n in range(pairs):
            part = slice(n * half, (n + 1) * half)
            tile = jnp.concatenate([turned[:cols, part], turned[cols:, part]], axis=1)
            for g in range(groups):
                send_ref[g * heads + place(mates, heads, h + n)] = tile


def prepare_kernel(block, pair_ref, inv_ref, var_s):
    halves, half, cols, chan = pair_ref.shape
    ones = jnp.full((16, chan), 1.0, BF16)
    for start in range(0, half, block):
        part = slice(start, start + block)
        cent = centred(pair_ref[:, part])
        for p, many, piece in pieces((cent * cent).astype(BF16), halves, block, cols):
            var = dot(ones, piece, NT)[:1] * (1.0 / chan)
            for n in range(many):
                var_s[pl.ds(start + p + n, 1), :] = var[:, n * halves * cols : (n + 1) * halves * cols]
    inv_ref[...] = lax.rsqrt(from_halves(var_s[...], cols) + EPS)


def attend_kernel(samples, wide, last, *refs):
    got_refs, refs = refs[:samples], refs[samples:]
    bias_ref, mask_ref, weight_ref, refs = refs[0], refs[1], refs[2], refs[3:]
    before_ref, refs = (None, refs) if len(refs) == samples + 5 else (refs[0], refs[1:])
    back_refs, refs = refs[:samples], refs[samples:]
    grad_ref, key_s, value_s, dk_s, dv_s = refs
    four, count = got_refs[0].shape
    dim = four // 4
    root = 1.0 / math.sqrt(dim)
    samp, heads, cols, rows = bias_ref.shape
    first = lax.broadcasted_iota(jnp.int32, (16, count), 0) == 0
    mask_rows = jnp.where(first & (mask_ref[...] <= 0), MASKED, 0.0).astype(BF16)
    one_rows = jnp.where(lax.broadcasted_iota(jnp.int32, (16, wide), 0) == 0, 1.0, 0.0).astype(BF16)
    for s, got_ref in enumerate(got_refs):
        keys = got_ref[dim : 2 * dim, :]
        key_s[s] = jnp.concatenate([keys, keys, mask_rows], axis=0).T
        value_s[s] = got_ref[2 * dim : 3 * dim, :].T
    per = wide // rows
    for a in range(count // wide):
        lanes = slice(a * wide, (a + 1) * wide)
        bias = jnp.concatenate(
            [bias_ref[:, a * per + p].reshape(count, rows) for p in range(per)], axis=1
        ).astype(F32) * LOG2E
        total = None if before_ref is None else before_ref[:, lanes]
        for s, (got_ref, back_ref) in enumerate(zip(got_refs, back_refs)):
            query = got_ref[0:dim, lanes]
            scaled = query.astype(F32) * (LOG2E * root)
            upper = scaled.astype(BF16)
            lower = (scaled - upper.astype(F32)).astype(BF16)
            scores = dot(key_s[s], jnp.concatenate([upper, lower, one_rows], axis=0)) + bias
            expo = jnp.exp2(scores - jnp.max(scores, axis=0, keepdims=True))
            inv_sum = 1.0 / jnp.sum(expo, axis=0, keepdims=True)
            expo_b = expo.astype(BF16)
            out = dot(got_ref[2 * dim : 3 * dim, :], expo_b) * inv_sum
            back_ref[0:dim, lanes] = out.astype(BF16)
            grad_in = (got_ref[3 * dim : 4 * dim, lanes].astype(F32) * weight_ref[:, lanes]).astype(BF16)
            grad = (grad_in.astype(F32) * inv_sum).astype(BF16)
            row_dot = jnp.sum(grad.astype(F32) * out, axis=0, keepdims=True)
            dscore = expo * (dot(value_s[s], grad) - row_dot)
            total = dscore if total is None else total + dscore
            dscore_b = dscore.astype(BF16)
            back_ref[dim : 2 * dim, lanes] = (dot(got_ref[dim : 2 * dim, :], dscore_b) * root).astype(BF16)
            dk = dot(query, dscore_b, NT)
            dv = dot(grad, expo_b, NT)
            if a == 0:
                dk_s[s] = dk
                dv_s[s] = dv
            else:
                dk_s[s] += dk
                dv_s[s] += dv
        if not last:
            grad_ref[:, lanes] = total
            continue
        total = total.astype(BF16)
        for p in range(per):
            grad_ref[:, a * per + p] = total[:, p * rows : (p + 1) * rows].reshape(samp, cols, rows)
    for s, back_ref in enumerate(back_refs):
        back_ref[2 * dim : 3 * dim, :] = (dk_s[s] * root).astype(BF16)
        back_ref[3 * dim : 4 * dim, :] = dv_s[s].astype(BF16)


def reduce_kernel(groups, mates, got_ref, inv_ref, pair_ref, sum_ref, plain_s):
    halves, half, cols, chan = pair_ref.shape
    devices, heads, _ = sum_ref.shape
    for h in range(heads):
        plain = gathered(groups, mates, heads, h, got_ref) * inv_ref[...]
        plain_s[h * half : (h + 1) * half, :] = to_halves(plain)
    total = jnp.zeros((heads, chan), F32)
    many = step_of(half, 8)
    for first in range(0, half, many):
        some = range(first, first + many)
        plain = jnp.concatenate([plain_s[pl.ds(p, heads, stride=half), :] for p in some], axis=1)
        total += dot(
            plain.astype(BF16), jnp.concatenate([pair_ref[h, p] for p in some for h in range(halves)], axis=0)
        )
    total = (total - jnp.mean(total, axis=1, keepdims=True)).astype(BF16)
    for n in range(devices):
        sum_ref[n] = total


def place(mates, heads, h):
    return (h % mates) * (heads // mates) + h // mates


def gathered(groups, mates, heads, h, got_ref):
    at = place(mates, heads, h)
    grad = got_ref[at].astype(F32)
    for g in range(1, groups):
        grad += got_ref[g * heads + at].astype(F32)
    return grad


def pair_kernel(
    groups, mates, block, got_ref, bias_ref, inv_ref, gain_ref, proj_ref, pair_ref, out_ref,
    out_s, sems, plain_s, biased_s,
):
    halves, half, cols, chan = pair_ref.shape
    heads = proj_ref.shape[0]
    outs = copies_of(out_s, out_ref, sems, block)
    scaled = proj_ref[...].astype(F32) * gain_ref[...]
    scaled = (scaled - jnp.mean(scaled, axis=1, keepdims=True)).astype(BF16)
    none = jnp.zeros((heads, chan), BF16)
    ones = jnp.ones((heads, chan), BF16)
    right = jnp.concatenate(
        [jnp.concatenate([scaled, none], axis=1), jnp.concatenate([none, ones], axis=1)], axis=0
    )
    inv_std = inv_ref[...]
    for h in range(heads):
        plain = gathered(groups, mates, heads, h, got_ref) * inv_std
        biased = plain * inv_std * bias_ref[place(mates, heads, h)].astype(F32) * (1.0 / chan)
        plain_s[h * half : (h + 1) * half, :] = to_halves(plain)
        biased_s[h * half : (h + 1) * half, :] = to_halves(biased)
    for step, copy in enumerate(outs):
        first = step * block
        cent = centred(pair_ref[:, first : first + block]).reshape(halves, block, cols, chan)
        for p in range(first, first + block):
            take = pl.ds(p, heads, stride=half)
            left = jnp.concatenate([plain_s[take, :], biased_s[take, :]], axis=0).astype(BF16)
            both = dot(left, right, TN)
            for h in range(halves):
                part = slice(h * cols, (h + 1) * cols)
                out_s[h, p] = (both[part, :chan] - cent[h, p - first] * both[part, chan:]).astype(BF16)
        copy.start()
    for copy in outs:
        copy.wait()


def final_kernel(scale, sums_ref, gain_ref, proj_ref, weight_ref, gain_grad_ref):
    total = sums_ref[0].astype(F32)
    for n in range(1, sums_ref.shape[0]):
        total += sums_ref[n].astype(F32)
    total = total * scale
    weight_ref[...] = total * gain_ref[...]
    gain_grad_ref[...] = jnp.sum(total * proj_ref[...].astype(F32), axis=0, keepdims=True)


def local(groups, mates, axes, queries, keys, values, out_grad, pair, ln_gain, proj_weight, token_mask, atom_map):
    _, width, count = queries.shape
    rows, cols, chan = pair.shape
    heads = proj_weight.shape[1]
    dim = width // mates
    head_parts = heads // mates
    devices = groups * mates * head_parts
    entries = rows * cols
    half = rows // 2
    gain_row = ln_gain.reshape(1, chan)
    proj_rows = proj_weight.T
    mask_row = token_mask.reshape(1, count)
    pair = pair.reshape(2, half, cols, chan)
    mate = lax.axis_index(axes[1]).astype(jnp.int32).reshape(1)
    whole = lambda *shape: pl.BlockSpec(shape, lambda *_: (0,) * len(shape))
    scalar = pl.BlockSpec(memory_space=pltpu.SMEM)
    vector = pl.BlockSpec(memory_space=pltpu.VMEM)

    def swap(chunks):
        return [
            lax.ppermute(x, axes[1], [(i, i ^ k) for i in range(mates)]) if k else x
            for k, x in enumerate(chunks)
        ]

    block = step_of(half, 16)
    far = pl.BlockSpec(memory_space=pltpu.HBM)
    tiles = jax.ShapeDtypeStruct((devices, cols, rows), BF16)
    by_head = pltpu.VMEM((heads * half, 2 * cols), F32)
    near = pltpu.VMEM(pair.shape, BF16)
    sems = pltpu.SemaphoreType.DMA((half // block,))

    chunks = (jax.ShapeDtypeStruct((4 * dim, count), BF16),) * mates
    send = call(
        functools.partial(pack_kernel, dim), "pack", 0, 16 * width * count, SMALL,
        out_shape=chunks,
        in_specs=[scalar] + [far] * 4,
        out_specs=(vector,) * mates,
        scratch_shapes=[pltpu.SemaphoreType.DMA((mates, 4))],
    )(mate, queries, keys, values, out_grad)
    got = swap(send)

    bias_send = call(
        functools.partial(norm_kernel, groups, mates, block), "norm", 2 * entries * chan * heads,
        2 * entries * chan, BIG,
        out_shape=tiles,
        in_specs=[vector] * 3,
        out_specs=vector,
        scratch_shapes=[by_head],
    )(pair, gain_row, proj_rows)
    bias = lax.all_to_all(bias_send, axes, 0, 0, tiled=True)

    weight = call(
        weight_kernel, "weight", 2 * 144 * atom_map.shape[0], 0, SMALL,
        out_shape=jax.ShapeDtypeStruct((1, count), F32),
    )(atom_map.reshape(1, -1), mask_row)

    fine = rows % 128 == 0
    samp = groups * mates
    bias = bias.reshape(samp, head_parts, cols, rows)
    if not fine:
        bias = bias.transpose(0, 2, 1, 3).reshape(1, 1, count, count)
    wide = max(rows, step_of(count, 512)) if fine else count
    order = sorted(range(mates), key=lambda k: ORDER.index(k) if k in ORDER else k)
    back, before = [None] * mates, ()
    for n in range(0, mates, SPLIT):
        part = order[n : n + SPLIT]
        many, last = len(part), n + SPLIT >= mates
        *outs, grads = call(
            functools.partial(attend_kernel, many, wide, last), "attend", 12 * many * dim * count * count,
            8 * many * dim * count * 2 + 4 * count * count, SMALL,
            out_shape=chunks[:many]
            + (jax.ShapeDtypeStruct(bias.shape, BF16) if last else jax.ShapeDtypeStruct((count, count), F32),),
            scratch_shapes=[
                pltpu.VMEM((many, count, 2 * dim + 16), BF16),
                pltpu.VMEM((many, count, dim), BF16),
                pltpu.VMEM((many, dim, count), F32),
                pltpu.VMEM((many, dim, count), F32),
            ],
        )(*[got[k] for k in part], bias, mask_row, weight, *before)
        before = (grads,)
        for k, x in zip(part, outs):
            back[k] = x
    if not fine:
        grads = grads.reshape(samp, cols, head_parts, rows).transpose(0, 2, 1, 3)
    swapped = swap(back)
    pair_later, swapped = together(pair, swapped, NEXT)
    inv_std = call(
        functools.partial(prepare_kernel, block), "prepare", 2 * entries * chan * heads, 2 * entries * chan, SMALL,
        out_shape=jax.ShapeDtypeStruct((cols, rows), F32),
        in_specs=[vector],
        out_specs=vector,
        scratch_shapes=[pltpu.VMEM((half, 2 * cols), F32)],
    )(pair_later)
    grads, swapped = together(grads, swapped, FIRST)
    grads = lax.all_to_all(grads.reshape(devices, cols, rows), axes, 0, 0, tiled=True)
    parts = call(
        functools.partial(reduce_kernel, groups, mates), "reduce", 2 * entries * chan * heads,
        2 * entries * chan, SMALL,
        out_shape=jax.ShapeDtypeStruct((devices, heads, chan), BF16),
        in_specs=[vector] * 3,
        out_specs=vector,
        scratch_shapes=[by_head],
    )(grads, inv_std, pair)
    parts, swapped = together(parts, swapped, EARLY)
    sums = lax.all_to_all(parts, axes, 0, 0, tiled=True)

    def unpacked(some, wholes):
        some = [k for k in some if k < mates]
        if not some:
            return wholes
        return call(
            functools.partial(unpack_kernel, some, dim), "unpack", 0, 16 * width * count, SMALL,
            out_shape=(jax.ShapeDtypeStruct(queries.shape, BF16),) * 4,
            in_specs=[scalar] + [vector] * len(some) + [far] * len(wholes),
            out_specs=(far,) * 4,
            scratch_shapes=[pltpu.SemaphoreType.DMA((len(some), 4))],
            input_output_aliases={1 + len(some) + n: n for n in range(len(wholes))},
        )(mate, *[swapped[k] for k in some], *wholes)

    wholes = unpacked([k for k in range(mates) if k not in LATE], ())
    grads, wholes = lax.optimization_barrier((grads, wholes))
    pair_grad = call(
        functools.partial(pair_kernel, groups, mates, block), "pair_grad", 8 * entries * chan * heads,
        4 * entries * chan, SMALL,
        out_shape=jax.ShapeDtypeStruct(pair.shape, BF16),
        in_specs=[vector] * 6,
        out_specs=far,
        scratch_shapes=[near, sems, by_head, by_head],
    )(grads, bias_send, inv_std, gain_row, proj_rows, pair)
    pair_grad, swapped = together(pair_grad, swapped, LATE)
    attended, query_grad, key_grad, value_grad = unpacked(LATE, wholes)
    weight_rows, gain_grad = call(
        functools.partial(final_kernel, 1.0 / count), "final", 0, 2 * devices * heads * chan, SMALL,
        out_shape=(
            jax.ShapeDtypeStruct((heads, chan), F32),
            jax.ShapeDtypeStruct((1, chan), F32),
        ),
    )(sums, gain_row, proj_rows)
    return (
        attended, query_grad, key_grad, value_grad,
        pair_grad.reshape(rows, cols, chan), weight_rows.T, gain_grad.reshape(chan),
    )


def solution(mesh):
    samp, head = mesh.axis_names
    samp_size, head_size = mesh.shape[samp], mesh.shape[head]

    def run(*args):
        heads = args[6].shape[1]
        mates = math.gcd(heads // head_size, samp_size)
        groups = samp_size // mates
        axes = ("group", "mate", "part")
        fine = Mesh(mesh.devices.reshape(groups, mates, head_size), axes)
        by_sample = P(("group", "mate"), "part", None)
        by_pair = P("part", ("group", "mate"), None)
        return jax.shard_map(
            functools.partial(local, groups, mates, axes),
            mesh=fine,
            in_specs=(by_sample,) * 4 + (by_pair,) + (P(),) * 4,
            out_specs=(by_sample,) * 4 + (by_pair, P(), P()),
            check_vma=False,
        )(*args)

    return run
```

```python
import functools
import math

import jax
import jax.numpy as jnp
from jax import lax
from jax.experimental import pallas as pl
from jax.experimental.pallas import tpu as pltpu
from jax.sharding import Mesh
from jax.sharding import PartitionSpec as P

F32 = jnp.float32
BF16 = jnp.bfloat16
LOG2E = math.log2(math.e)
EPS = 1e-05
MASKED = -1000000000.0
BIG = 60
SMALL = 24
SPLIT = 1
ORDER = (0, 1, 2, 3)
FIRST = ()
NEXT = ()
EARLY = (3,)
LATE = (1, 2)
NT = (((1,), (1,)), ((), ()))
TN = (((0,), (0,)), ((), ()))


def dot(a, b, dims=(((1,), (0,)), ((), ()))):
    return lax.dot_general(a, b, dims, preferred_element_type=F32)


def call(kernel, name, flops, moved, mebi, **kw):
    return pl.pallas_call(
        kernel,
        name=name,
        compiler_params=pltpu.CompilerParams(vmem_limit_bytes=mebi * 1024 * 1024),
        cost_estimate=pl.CostEstimate(flops=flops, bytes_accessed=moved, transcendentals=0),
        **kw,
    )


def together(value, chunks, some):
    some = [k for k in some if k < len(chunks)]
    if not some:
        return value, chunks
    value, taken = lax.optimization_barrier((value, [chunks[k] for k in some]))
    return value, [taken[some.index(k)] if k in some else x for k, x in enumerate(chunks)]


def step_of(count, most):
    return max(n for n in range(1, most + 1) if count % n == 0)


def head_part(mate_ref, k, dim):
    return pl.ds(pl.multiple_of(jnp.bitwise_xor(mate_ref[0], k) * dim, 16), dim)


def pack_kernel(dim, mate_ref, *refs):
    from_refs, send_refs, sems = refs[:4], refs[4:-1], refs[-1]
    copies = [
        pltpu.make_async_copy(
            from_ref.at[0, head_part(mate_ref, k, dim)], send_ref.at[n * dim : (n + 1) * dim], sems.at[k, n]
        )
        for k, send_ref in enumerate(send_refs)
        for n, from_ref in enumerate(from_refs)
    ]
    for copy in copies:
        copy.start()
    for copy in copies:
        copy.wait()


def unpack_copies(some, dim, mate_ref, got_refs, out_refs, sems):
    return [
        pltpu.make_async_copy(
            got_ref.at[n * dim : (n + 1) * dim], out_ref.at[0, head_part(mate_ref, k, dim)], sems.at[m, n]
        )
        for m, (k, got_ref) in enumerate(zip(some, got_refs))
        for n, out_ref in enumerate(out_refs)
    ]


def unpack_kernel(some, dim, mate_ref, *refs):
    copies = unpack_copies(some, dim, mate_ref, refs[: len(some)], refs[-5:-1], refs[-1])
    for copy in copies:
        copy.start()
    for copy in copies:
        copy.wait()


def weight_kernel(map_ref, mask_ref, weight_ref):
    count = mask_ref.shape[1]
    atoms = map_ref.shape[1]
    rows = pl.cdiv(count, 128)
    tall = pl.cdiv(rows, 16) * 16
    token = map_ref[...]
    high = lax.shift_right_logical(token, 7)
    low = jnp.bitwise_and(token, 127)
    is_row = (lax.broadcasted_iota(jnp.int32, (tall, atoms), 0) == high).astype(F32).astype(BF16)
    is_lane = (lax.broadcasted_iota(jnp.int32, (128, atoms), 0) == low).astype(F32).astype(BF16)
    counts = dot(is_row, is_lane, NT)
    line = jnp.concatenate([counts[r : r + 1, :] for r in range(rows)], axis=1)[:, :count]
    weight_ref[...] = line * (count / atoms) * mask_ref[...].astype(F32)


def copies_of(near_ref, far_ref, sems, block):
    return [
        pltpu.make_async_copy(near_ref.at[:, pl.ds(p, block)], far_ref.at[:, pl.ds(p, block)], sems.at[n])
        for n, p in enumerate(range(0, near_ref.shape[1], block))
    ]


def centred(pair):
    halves, block, cols, chan = pair.shape
    rows = pair.reshape(halves * block * cols, chan)
    return rows.astype(F32) - dot(rows, jnp.full((chan, chan), 1.0, BF16)) * (1.0 / chan)


def pieces(values, halves, block, cols):
    many = 2 if block % 2 == 0 else 1
    for p in range(0, block, many):
        starts = [(h * block + p + n) * cols for n in range(many) for h in range(halves)]
        yield p, many, jnp.concatenate([values[x : x + cols] for x in starts], axis=0)


def from_halves(block, cols):
    turned = block.T
    return jnp.concatenate([turned[:cols], turned[cols:]], axis=1)


def to_halves(block):
    half = block.shape[1] // 2
    return jnp.concatenate([block[:, :half], block[:, half:]], axis=0).T


def norm_kernel(groups, mates, block, pair_ref, gain_ref, proj_ref, send_ref, bias_s):
    halves, half, cols, chan = pair_ref.shape
    heads = proj_ref.shape[0]
    for first in range(0, half, block):
        cent = centred(pair_ref[:, first : first + block])
        inv_std = lax.rsqrt(jnp.mean(cent * cent, axis=-1, keepdims=True) + EPS)
        lnout = (cent * inv_std * gain_ref[...]).astype(BF16)
        for p, many, piece in pieces(lnout, halves, block, cols):
            bias = dot(proj_ref[...], piece, NT)
            for n in range(many):
                bias_s[pl.ds(first + p + n, heads, stride=half), :] = bias[
                    :, n * halves * cols : (n + 1) * halves * cols
                ]
    pairs = 2 if heads % 2 == 0 else 1
    for h in range(0, heads, pairs):
        turned = bias_s[h * half : (h + pairs) * half, :].T.astype(BF16)
        for n in range(pairs):
            part = slice(n * half, (n + 1) * half)
            tile = jnp.concatenate([turned[:cols, part], turned[cols:, part]], axis=1)
            for g in range(groups):
                send_ref[g * heads + place(mates, heads, h + n)] = tile


def prepare_kernel(block, pair_ref, inv_ref, var_s):
    halves, half, cols, chan = pair_ref.shape
    ones = jnp.full((16, chan), 1.0, BF16)
    for start in range(0, half, block):
        part = slice(start, start + block)
        cent = centred(pair_ref[:, part])
        for p, many, piece in pieces((cent * cent).astype(BF16), halves, block, cols):
            var = dot(ones, piece, NT)[:1] * (1.0 / chan)
            for n in range(many):
                var_s[pl.ds(start + p + n, 1), :] = var[:, n * halves * cols : (n + 1) * halves * cols]
    inv_ref[...] = lax.rsqrt(from_halves(var_s[...], cols) + EPS)


def attend_kernel(samples, wide, last, *refs):
    got_refs, refs = refs[:samples], refs[samples:]
    bias_ref, mask_ref, weight_ref, refs = refs[0], refs[1], refs[2], refs[3:]
    before_ref, refs = (None, refs) if len(refs) == samples + 5 else (refs[0], refs[1:])
    back_refs, refs = refs[:samples], refs[samples:]
    grad_ref, key_s, value_s, dk_s, dv_s = refs
    four, count = got_refs[0].shape
    dim = four // 4
    root = 1.0 / math.sqrt(dim)
    samp, heads, cols, rows = bias_ref.shape
    first = lax.broadcasted_iota(jnp.int32, (16, count), 0) == 0
    mask_rows = jnp.where(first & (mask_ref[...] <= 0), MASKED, 0.0).astype(BF16)
    one_rows = jnp.where(lax.broadcasted_iota(jnp.int32, (16, wide), 0) == 0, 1.0, 0.0).astype(BF16)
    for s, got_ref in enumerate(got_refs):
        keys = got_ref[dim : 2 * dim, :]
        key_s[s] = jnp.concatenate([keys, keys, mask_rows], axis=0).T
        value_s[s] = got_ref[2 * dim : 3 * dim, :].T
    per = wide // rows
    for a in range(count // wide):
        lanes = slice(a * wide, (a + 1) * wide)
        bias = jnp.concatenate(
            [bias_ref[:, a * per + p].reshape(count, rows) for p in range(per)], axis=1
        ).astype(F32) * LOG2E
        total = None if before_ref is None else before_ref[:, lanes]
        for s, (got_ref, back_ref) in enumerate(zip(got_refs, back_refs)):
            query = got_ref[0:dim, lanes]
            scaled = query.astype(F32) * (LOG2E * root)
            upper = scaled.astype(BF16)
            lower = (scaled - upper.astype(F32)).astype(BF16)
            scores = dot(key_s[s], jnp.concatenate([upper, lower, one_rows], axis=0)) + bias
            expo = jnp.exp2(scores - jnp.max(scores, axis=0, keepdims=True))
            inv_sum = 1.0 / jnp.sum(expo, axis=0, keepdims=True)
            expo_b = expo.astype(BF16)
            out = dot(got_ref[2 * dim : 3 * dim, :], expo_b) * inv_sum
            back_ref[0:dim, lanes] = out.astype(BF16)
            grad_in = (got_ref[3 * dim : 4 * dim, lanes].astype(F32) * weight_ref[:, lanes]).astype(BF16)
            grad = (grad_in.astype(F32) * inv_sum).astype(BF16)
            row_dot = jnp.sum(grad.astype(F32) * out, axis=0, keepdims=True)
            dscore = expo * (dot(value_s[s], grad) - row_dot)
            total = dscore if total is None else total + dscore
            dscore_b = dscore.astype(BF16)
            back_ref[dim : 2 * dim, lanes] = (dot(got_ref[dim : 2 * dim, :], dscore_b) * root).astype(BF16)
            dk = dot(query, dscore_b, NT)
            dv = dot(grad, expo_b, NT)
            if a == 0:
                dk_s[s] = dk
                dv_s[s] = dv
            else:
                dk_s[s] += dk
                dv_s[s] += dv
        if not last:
            grad_ref[:, lanes] = total
            continue
        total = total.astype(BF16)
        for p in range(per):
            grad_ref[:, a * per + p] = total[:, p * rows : (p + 1) * rows].reshape(samp, cols, rows)
    for s, back_ref in enumerate(back_refs):
        back_ref[2 * dim : 3 * dim, :] = (dk_s[s] * root).astype(BF16)
        back_ref[3 * dim : 4 * dim, :] = dv_s[s].astype(BF16)


def reduce_kernel(groups, mates, got_ref, inv_ref, pair_ref, sum_ref, plain_s):
    halves, half, cols, chan = pair_ref.shape
    devices, heads, _ = sum_ref.shape
    for h in range(heads):
        plain = gathered(groups, mates, heads, h, got_ref) * inv_ref[...]
        plain_s[h * half : (h + 1) * half, :] = to_halves(plain)
    total = jnp.zeros((heads, chan), F32)
    many = step_of(half, 8)
    for first in range(0, half, many):
        some = range(first, first + many)
        plain = jnp.concatenate([plain_s[pl.ds(p, heads, stride=half), :] for p in some], axis=1)
        total += dot(
            plain.astype(BF16), jnp.concatenate([pair_ref[h, p] for p in some for h in range(halves)], axis=0)
        )
    total = (total - jnp.mean(total, axis=1, keepdims=True)).astype(BF16)
    for n in range(devices):
        sum_ref[n] = total


def place(mates, heads, h):
    return (h % mates) * (heads // mates) + h // mates


def gathered(groups, mates, heads, h, got_ref):
    at = place(mates, heads, h)
    grad = got_ref[at].astype(F32)
    for g in range(1, groups):
        grad += got_ref[g * heads + at].astype(F32)
    return grad


def pair_kernel(groups, mates, block, some, dim, mate_ref, *refs):
    chunk_refs, refs = refs[: len(some)], refs[len(some) :]
    got_ref, bias_ref, inv_ref, gain_ref, proj_ref, pair_ref, out_ref, *refs = refs
    *whole_refs, out_s, sems, plain_s, biased_s, chunk_sems = refs
    chunks = unpack_copies(some, dim, mate_ref, chunk_refs, whole_refs, chunk_sems)
    for copy in chunks:
        copy.start()
    halves, half, cols, chan = pair_ref.shape
    heads = proj_ref.shape[0]
    outs = copies_of(out_s, out_ref, sems, block)
    scaled = proj_ref[...].astype(F32) * gain_ref[...]
    scaled = (scaled - jnp.mean(scaled, axis=1, keepdims=True)).astype(BF16)
    none = jnp.zeros((heads, chan), BF16)
    ones = jnp.ones((heads, chan), BF16)
    right = jnp.concatenate(
        [jnp.concatenate([scaled, none], axis=1), jnp.concatenate([none, ones], axis=1)], axis=0
    )
    inv_std = inv_ref[...]
    for h in range(heads):
        plain = gathered(groups, mates, heads, h, got_ref) * inv_std
        biased = plain * inv_std * bias_ref[place(mates, heads, h)].astype(F32) * (1.0 / chan)
        plain_s[h * half : (h + 1) * half, :] = to_halves(plain)
        biased_s[h * half : (h + 1) * half, :] = to_halves(biased)
    for step, copy in enumerate(outs):
        first = step * block
        cent = centred(pair_ref[:, first : first + block]).reshape(halves, block, cols, chan)
        for p in range(first, first + block):
            take = pl.ds(p, heads, stride=half)
            left = jnp.concatenate([plain_s[take, :], biased_s[take, :]], axis=0).astype(BF16)
            both = dot(left, right, TN)
            for h in range(halves):
                part = slice(h * cols, (h + 1) * cols)
                out_s[h, p] = (both[part, :chan] - cent[h, p - first] * both[part, chan:]).astype(BF16)
        copy.start()
    for copy in outs + chunks:
        copy.wait()


def final_kernel(scale, sums_ref, gain_ref, proj_ref, weight_ref, gain_grad_ref):
    total = sums_ref[0].astype(F32)
    for n in range(1, sums_ref.shape[0]):
        total += sums_ref[n].astype(F32)
    total = total * scale
    weight_ref[...] = total * gain_ref[...]
    gain_grad_ref[...] = jnp.sum(total * proj_ref[...].astype(F32), axis=0, keepdims=True)


def local(groups, mates, axes, queries, keys, values, out_grad, pair, ln_gain, proj_weight, token_mask, atom_map):
    _, width, count = queries.shape
    rows, cols, chan = pair.shape
    heads = proj_weight.shape[1]
    dim = width // mates
    head_parts = heads // mates
    devices = groups * mates * head_parts
    entries = rows * cols
    half = rows // 2
    gain_row = ln_gain.reshape(1, chan)
    proj_rows = proj_weight.T
    mask_row = token_mask.reshape(1, count)
    pair = pair.reshape(2, half, cols, chan)
    mate = lax.axis_index(axes[1]).astype(jnp.int32).reshape(1)
    whole = lambda *shape: pl.BlockSpec(shape, lambda *_: (0,) * len(shape))
    scalar = pl.BlockSpec(memory_space=pltpu.SMEM)
    vector = pl.BlockSpec(memory_space=pltpu.VMEM)

    def swap(chunks):
        return [
            lax.ppermute(x, axes[1], [(i, i ^ k) for i in range(mates)]) if k else x
            for k, x in enumerate(chunks)
        ]

    block = step_of(half, 16)
    far = pl.BlockSpec(memory_space=pltpu.HBM)
    tiles = jax.ShapeDtypeStruct((devices, cols, rows), BF16)
    by_head = pltpu.VMEM(((heads + 1) * half, 2 * cols), F32)
    near = pltpu.VMEM(pair.shape, BF16)
    sems = pltpu.SemaphoreType.DMA((half // block,))

    chunks = (jax.ShapeDtypeStruct((4 * dim, count), BF16),) * mates
    send = call(
        functools.partial(pack_kernel, dim), "pack", 0, 16 * width * count, SMALL,
        out_shape=chunks,
        in_specs=[scalar] + [far] * 4,
        out_specs=(vector,) * mates,
        scratch_shapes=[pltpu.SemaphoreType.DMA((mates, 4))],
    )(mate, queries, keys, values, out_grad)
    got = swap(send)

    bias_send = call(
        functools.partial(norm_kernel, groups, mates, block), "norm", 2 * entries * chan * heads,
        2 * entries * chan, BIG,
        out_shape=tiles,
        in_specs=[vector] * 3,
        out_specs=vector,
        scratch_shapes=[by_head],
    )(pair, gain_row, proj_rows)
    bias = lax.all_to_all(bias_send, axes, 0, 0, tiled=True)

    weight = call(
        weight_kernel, "weight", 2 * 144 * atom_map.shape[0], 0, SMALL,
        out_shape=jax.ShapeDtypeStruct((1, count), F32),
    )(atom_map.reshape(1, -1), mask_row)

    fine = rows % 128 == 0
    samp = groups * mates
    bias = bias.reshape(samp, head_parts, cols, rows)
    if not fine:
        bias = bias.transpose(0, 2, 1, 3).reshape(1, 1, count, count)
    wide = max(rows, step_of(count, 512)) if fine else count
    order = sorted(range(mates), key=lambda k: ORDER.index(k) if k in ORDER else k)
    back, before = [None] * mates, ()
    for n in range(0, mates, SPLIT):
        part = order[n : n + SPLIT]
        many, last = len(part), n + SPLIT >= mates
        *outs, grads = call(
            functools.partial(attend_kernel, many, wide, last), "attend", 12 * many * dim * count * count,
            8 * many * dim * count * 2 + 4 * count * count, SMALL,
            out_shape=chunks[:many]
            + (jax.ShapeDtypeStruct(bias.shape, BF16) if last else jax.ShapeDtypeStruct((count, count), F32),),
            scratch_shapes=[
                pltpu.VMEM((many, count, 2 * dim + 16), BF16),
                pltpu.VMEM((many, count, dim), BF16),
                pltpu.VMEM((many, dim, count), F32),
                pltpu.VMEM((many, dim, count), F32),
            ],
        )(*[got[k] for k in part], bias, mask_row, weight, *before)
        before = (grads,)
        for k, x in zip(part, outs):
            back[k] = x
    if not fine:
        grads = grads.reshape(samp, cols, head_parts, rows).transpose(0, 2, 1, 3)
    swapped = swap(back)
    pair_later, swapped = together(pair, swapped, NEXT)
    inv_std = call(
        functools.partial(prepare_kernel, block), "prepare", 2 * entries * chan * heads, 2 * entries * chan, SMALL,
        out_shape=jax.ShapeDtypeStruct((cols, rows), F32),
        in_specs=[vector],
        out_specs=vector,
        scratch_shapes=[pltpu.VMEM((half, 2 * cols), F32)],
    )(pair_later)
    grads, swapped = together(grads, swapped, FIRST)
    grads = lax.all_to_all(grads.reshape(devices, cols, rows), axes, 0, 0, tiled=True)
    parts = call(
        functools.partial(reduce_kernel, groups, mates), "reduce", 2 * entries * chan * heads,
        2 * entries * chan, SMALL,
        out_shape=jax.ShapeDtypeStruct((devices, heads, chan), BF16),
        in_specs=[vector] * 3,
        out_specs=vector,
        scratch_shapes=[by_head],
    )(grads, inv_std, pair)
    parts, swapped = together(parts, swapped, EARLY)
    sums = lax.all_to_all(parts, axes, 0, 0, tiled=True)

    early, late = [k for k in range(mates) if k not in LATE], [k for k in LATE if k < mates]
    whole_outs = (jax.ShapeDtypeStruct(queries.shape, BF16),) * 4
    pair_grad, *wholes = call(
        functools.partial(pair_kernel, groups, mates, block, early, dim), "pair_grad", 8 * entries * chan * heads,
        4 * entries * chan, SMALL,
        out_shape=(jax.ShapeDtypeStruct(pair.shape, BF16),) + whole_outs,
        in_specs=[scalar] + [vector] * (len(early) + 6),
        out_specs=(far,) * 5,
        scratch_shapes=[near, sems, by_head, by_head, pltpu.SemaphoreType.DMA((len(early), 4))],
    )(mate, *[swapped[k] for k in early], grads, bias_send, inv_std, gain_row, proj_rows, pair)
    pair_grad, swapped = together(pair_grad, swapped, LATE)
    if late:
        wholes = call(
            functools.partial(unpack_kernel, late, dim), "unpack", 0, 16 * width * count, SMALL,
            out_shape=whole_outs,
            in_specs=[scalar] + [vector] * len(late) + [far] * 4,
            out_specs=(far,) * 4,
            scratch_shapes=[pltpu.SemaphoreType.DMA((len(late), 4))],
            input_output_aliases={1 + len(late) + n: n for n in range(4)},
        )(mate, *[swapped[k] for k in late], *wholes)
    attended, query_grad, key_grad, value_grad = wholes
    weight_rows, gain_grad = call(
        functools.partial(final_kernel, 1.0 / count), "final", 0, 2 * devices * heads * chan, SMALL,
        out_shape=(
            jax.ShapeDtypeStruct((heads, chan), F32),
            jax.ShapeDtypeStruct((1, chan), F32),
        ),
    )(sums, gain_row, proj_rows)
    return (
        attended, query_grad, key_grad, value_grad,
        pair_grad.reshape(rows, cols, chan), weight_rows.T, gain_grad.reshape(chan),
    )


def solution(mesh):
    samp, head = mesh.axis_names
    samp_size, head_size = mesh.shape[samp], mesh.shape[head]

    def run(*args):
        heads = args[6].shape[1]
        mates = math.gcd(heads // head_size, samp_size)
        groups = samp_size // mates
        axes = ("group", "mate", "part")
        fine = Mesh(mesh.devices.reshape(groups, mates, head_size), axes)
        by_sample = P(("group", "mate"), "part", None)
        by_pair = P("part", ("group", "mate"), None)
        return jax.shard_map(
            functools.partial(local, groups, mates, axes),
            mesh=fine,
            in_specs=(by_sample,) * 4 + (by_pair,) + (P(),) * 4,
            out_specs=(by_sample,) * 4 + (by_pair, P(), P()),
            check_vma=False,
        )(*args)

    return run
```

```python
import functools
import math

import jax
import jax.numpy as jnp
from jax import lax
from jax.experimental import pallas as pl
from jax.experimental.pallas import tpu as pltpu
from jax.sharding import Mesh
from jax.sharding import PartitionSpec as P

F32 = jnp.float32
BF16 = jnp.bfloat16
LOG2E = math.log2(math.e)
EPS = 1e-05
MASKED = -1000000000.0
BIG = 60
SMALL = 24
SPLIT = 1
ORDER = (0, 2, 1, 3)
FIRST = ()
NEXT = ()
EARLY = (3,)
LATE = (1, 2)
NT = (((1,), (1,)), ((), ()))
TN = (((0,), (0,)), ((), ()))


def dot(a, b, dims=(((1,), (0,)), ((), ()))):
    return lax.dot_general(a, b, dims, preferred_element_type=F32)


def call(kernel, name, flops, moved, mebi, **kw):
    return pl.pallas_call(
        kernel,
        name=name,
        compiler_params=pltpu.CompilerParams(vmem_limit_bytes=mebi * 1024 * 1024),
        cost_estimate=pl.CostEstimate(flops=flops, bytes_accessed=moved, transcendentals=0),
        **kw,
    )


def together(value, chunks, some):
    some = [k for k in some if k < len(chunks)]
    if not some:
        return value, chunks
    value, taken = lax.optimization_barrier((value, [chunks[k] for k in some]))
    return value, [taken[some.index(k)] if k in some else x for k, x in enumerate(chunks)]


def step_of(count, most):
    return max(n for n in range(1, most + 1) if count % n == 0)


def head_part(mate_ref, k, dim):
    return pl.ds(pl.multiple_of(jnp.bitwise_xor(mate_ref[0], k) * dim, 16), dim)


def pack_kernel(dim, mate_ref, *refs):
    from_refs, send_refs, sems = refs[:4], refs[4:-1], refs[-1]
    copies = [
        pltpu.make_async_copy(
            from_ref.at[0, head_part(mate_ref, k, dim)], send_ref.at[n * dim : (n + 1) * dim], sems.at[k, n]
        )
        for k, send_ref in enumerate(send_refs)
        for n, from_ref in enumerate(from_refs)
    ]
    for copy in copies:
        copy.start()
    for copy in copies:
        copy.wait()


def unpack_copies(some, dim, mate_ref, got_refs, out_refs, sems):
    return [
        pltpu.make_async_copy(
            got_ref.at[n * dim : (n + 1) * dim], out_ref.at[0, head_part(mate_ref, k, dim)], sems.at[m, n]
        )
        for m, (k, got_ref) in enumerate(zip(some, got_refs))
        for n, out_ref in enumerate(out_refs)
    ]


def unpack_kernel(some, dim, mate_ref, *refs):
    copies = unpack_copies(some, dim, mate_ref, refs[: len(some)], refs[-5:-1], refs[-1])
    for copy in copies:
        copy.start()
    for copy in copies:
        copy.wait()


def weight_kernel(map_ref, mask_ref, weight_ref):
    count = mask_ref.shape[1]
    atoms = map_ref.shape[1]
    rows = pl.cdiv(count, 128)
    tall = pl.cdiv(rows, 16) * 16
    token = map_ref[...]
    high = lax.shift_right_logical(token, 7)
    low = jnp.bitwise_and(token, 127)
    is_row = (lax.broadcasted_iota(jnp.int32, (tall, atoms), 0) == high).astype(F32).astype(BF16)
    is_lane = (lax.broadcasted_iota(jnp.int32, (128, atoms), 0) == low).astype(F32).astype(BF16)
    counts = dot(is_row, is_lane, NT)
    line = jnp.concatenate([counts[r : r + 1, :] for r in range(rows)], axis=1)[:, :count]
    weight_ref[...] = line * (count / atoms) * mask_ref[...].astype(F32)


def copies_of(near_ref, far_ref, sems, block):
    return [
        pltpu.make_async_copy(near_ref.at[:, pl.ds(p, block)], far_ref.at[:, pl.ds(p, block)], sems.at[n])
        for n, p in enumerate(range(0, near_ref.shape[1], block))
    ]


def centred(pair):
    halves, block, cols, chan = pair.shape
    rows = pair.reshape(halves * block * cols, chan)
    return rows.astype(F32) - dot(rows, jnp.full((chan, chan), 1.0, BF16)) * (1.0 / chan)


def pieces(values, halves, block, cols):
    many = 2 if block % 2 == 0 else 1
    for p in range(0, block, many):
        starts = [(h * block + p + n) * cols for n in range(many) for h in range(halves)]
        yield p, many, jnp.concatenate([values[x : x + cols] for x in starts], axis=0)


def from_halves(block, cols):
    turned = block.T
    return jnp.concatenate([turned[:cols], turned[cols:]], axis=1)


def to_halves(block):
    half = block.shape[1] // 2
    return jnp.concatenate([block[:, :half], block[:, half:]], axis=0).T


def norm_kernel(groups, mates, block, pair_ref, gain_ref, proj_ref, send_ref, bias_s):
    halves, half, cols, chan = pair_ref.shape
    heads = proj_ref.shape[0]
    for first in range(0, half, block):
        cent = centred(pair_ref[:, first : first + block])
        inv_std = lax.rsqrt(jnp.mean(cent * cent, axis=-1, keepdims=True) + EPS)
        lnout = (cent * inv_std * gain_ref[...]).astype(BF16)
        for p, many, piece in pieces(lnout, halves, block, cols):
            bias = dot(proj_ref[...], piece, NT)
            for n in range(many):
                bias_s[pl.ds(first + p + n, heads, stride=half), :] = bias[
                    :, n * halves * cols : (n + 1) * halves * cols
                ]
    pairs = 2 if heads % 2 == 0 else 1
    for h in range(0, heads, pairs):
        turned = bias_s[h * half : (h + pairs) * half, :].T.astype(BF16)
        for n in range(pairs):
            part = slice(n * half, (n + 1) * half)
            tile = jnp.concatenate([turned[:cols, part], turned[cols:, part]], axis=1)
            for g in range(groups):
                send_ref[g * heads + place(mates, heads, h + n)] = tile


def prepare_kernel(block, pair_ref, inv_ref, var_s):
    halves, half, cols, chan = pair_ref.shape
    ones = jnp.full((16, chan), 1.0, BF16)
    for start in range(0, half, block):
        part = slice(start, start + block)
        cent = centred(pair_ref[:, part])
        for p, many, piece in pieces((cent * cent).astype(BF16), halves, block, cols):
            var = dot(ones, piece, NT)[:1] * (1.0 / chan)
            for n in range(many):
                var_s[pl.ds(start + p + n, 1), :] = var[:, n * halves * cols : (n + 1) * halves * cols]
    inv_ref[...] = lax.rsqrt(from_halves(var_s[...], cols) + EPS)


def attend_kernel(samples, wide, last, *refs):
    got_refs, refs = refs[:samples], refs[samples:]
    bias_ref, mask_ref, weight_ref, refs = refs[0], refs[1], refs[2], refs[3:]
    before_ref, refs = (None, refs) if len(refs) == samples + 5 else (refs[0], refs[1:])
    back_refs, refs = refs[:samples], refs[samples:]
    grad_ref, key_s, value_s, dk_s, dv_s = refs
    four, count = got_refs[0].shape
    dim = four // 4
    root = 1.0 / math.sqrt(dim)
    samp, heads, cols, rows = bias_ref.shape
    first = lax.broadcasted_iota(jnp.int32, (16, count), 0) == 0
    mask_rows = jnp.where(first & (mask_ref[...] <= 0), MASKED, 0.0).astype(BF16)
    one_rows = jnp.where(lax.broadcasted_iota(jnp.int32, (16, wide), 0) == 0, 1.0, 0.0).astype(BF16)
    for s, got_ref in enumerate(got_refs):
        keys = got_ref[dim : 2 * dim, :]
        key_s[s] = jnp.concatenate([keys, keys, mask_rows], axis=0).T
        value_s[s] = got_ref[2 * dim : 3 * dim, :].T
    per = wide // rows
    for a in range(count // wide):
        lanes = slice(a * wide, (a + 1) * wide)
        bias = jnp.concatenate(
            [bias_ref[:, a * per + p].reshape(count, rows) for p in range(per)], axis=1
        ).astype(F32) * LOG2E
        total = None if before_ref is None else before_ref[:, lanes]
        for s, (got_ref, back_ref) in enumerate(zip(got_refs, back_refs)):
            query = got_ref[0:dim, lanes]
            scaled = query.astype(F32) * (LOG2E * root)
            upper = scaled.astype(BF16)
            lower = (scaled - upper.astype(F32)).astype(BF16)
            scores = dot(key_s[s], jnp.concatenate([upper, lower, one_rows], axis=0)) + bias
            expo = jnp.exp2(scores - jnp.max(scores, axis=0, keepdims=True))
            inv_sum = 1.0 / jnp.sum(expo, axis=0, keepdims=True)
            expo_b = expo.astype(BF16)
            out = dot(got_ref[2 * dim : 3 * dim, :], expo_b) * inv_sum
            back_ref[0:dim, lanes] = out.astype(BF16)
            grad_in = (got_ref[3 * dim : 4 * dim, lanes].astype(F32) * weight_ref[:, lanes]).astype(BF16)
            grad = (grad_in.astype(F32) * inv_sum).astype(BF16)
            row_dot = jnp.sum(grad.astype(F32) * out, axis=0, keepdims=True)
            dscore = expo * (dot(value_s[s], grad) - row_dot)
            total = dscore if total is None else total + dscore
            dscore_b = dscore.astype(BF16)
            back_ref[dim : 2 * dim, lanes] = (dot(got_ref[dim : 2 * dim, :], dscore_b) * root).astype(BF16)
            dk = dot(query, dscore_b, NT)
            dv = dot(grad, expo_b, NT)
            if a == 0:
                dk_s[s] = dk
                dv_s[s] = dv
            else:
                dk_s[s] += dk
                dv_s[s] += dv
        if not last:
            grad_ref[:, lanes] = total
            continue
        total = total.astype(BF16)
        for p in range(per):
            grad_ref[:, a * per + p] = total[:, p * rows : (p + 1) * rows].reshape(samp, cols, rows)
    for s, back_ref in enumerate(back_refs):
        back_ref[2 * dim : 3 * dim, :] = (dk_s[s] * root).astype(BF16)
        back_ref[3 * dim : 4 * dim, :] = dv_s[s].astype(BF16)


def reduce_kernel(groups, mates, got_ref, inv_ref, pair_ref, sum_ref, plain_s):
    halves, half, cols, chan = pair_ref.shape
    devices, heads, _ = sum_ref.shape
    for h in range(heads):
        plain = gathered(groups, mates, heads, h, got_ref) * inv_ref[...]
        plain_s[h * half : (h + 1) * half, :] = to_halves(plain)
    total = jnp.zeros((heads, chan), F32)
    many = step_of(half, 8)
    for first in range(0, half, many):
        some = range(first, first + many)
        plain = jnp.concatenate([plain_s[pl.ds(p, heads, stride=half), :] for p in some], axis=1)
        total += dot(
            plain.astype(BF16), jnp.concatenate([pair_ref[h, p] for p in some for h in range(halves)], axis=0)
        )
    total = (total - jnp.mean(total, axis=1, keepdims=True)).astype(BF16)
    for n in range(devices):
        sum_ref[n] = total


def place(mates, heads, h):
    return (h % mates) * (heads // mates) + h // mates


def gathered(groups, mates, heads, h, got_ref):
    at = place(mates, heads, h)
    grad = got_ref[at].astype(F32)
    for g in range(1, groups):
        grad += got_ref[g * heads + at].astype(F32)
    return grad


def pair_kernel(groups, mates, block, some, dim, mate_ref, *refs):
    chunk_refs, refs = refs[: len(some)], refs[len(some) :]
    got_ref, bias_ref, inv_ref, gain_ref, proj_ref, pair_ref, out_ref, *refs = refs
    *whole_refs, out_s, sems, plain_s, biased_s, chunk_sems = refs
    chunks = unpack_copies(some, dim, mate_ref, chunk_refs, whole_refs, chunk_sems)
    for copy in chunks:
        copy.start()
    halves, half, cols, chan = pair_ref.shape
    heads = proj_ref.shape[0]
    outs = copies_of(out_s, out_ref, sems, block)
    scaled = proj_ref[...].astype(F32) * gain_ref[...]
    scaled = (scaled - jnp.mean(scaled, axis=1, keepdims=True)).astype(BF16)
    none = jnp.zeros((heads, chan), BF16)
    ones = jnp.ones((heads, chan), BF16)
    right = jnp.concatenate(
        [jnp.concatenate([scaled, none], axis=1), jnp.concatenate([none, ones], axis=1)], axis=0
    )
    inv_std = inv_ref[...]
    for h in range(heads):
        plain = gathered(groups, mates, heads, h, got_ref) * inv_std
        biased = plain * inv_std * bias_ref[place(mates, heads, h)].astype(F32) * (1.0 / chan)
        plain_s[h * half : (h + 1) * half, :] = to_halves(plain)
        biased_s[h * half : (h + 1) * half, :] = to_halves(biased)
    for step, copy in enumerate(outs):
        first = step * block
        cent = centred(pair_ref[:, first : first + block]).reshape(halves, block, cols, chan)
        for p in range(first, first + block):
            take = pl.ds(p, heads, stride=half)
            left = jnp.concatenate([plain_s[take, :], biased_s[take, :]], axis=0).astype(BF16)
            both = dot(left, right, TN)
            for h in range(halves):
                part = slice(h * cols, (h + 1) * cols)
                out_s[h, p] = (both[part, :chan] - cent[h, p - first] * both[part, chan:]).astype(BF16)
        copy.start()
    for copy in outs + chunks:
        copy.wait()


def final_kernel(scale, sums_ref, gain_ref, proj_ref, weight_ref, gain_grad_ref):
    total = sums_ref[0].astype(F32)
    for n in range(1, sums_ref.shape[0]):
        total += sums_ref[n].astype(F32)
    total = total * scale
    weight_ref[...] = total * gain_ref[...]
    gain_grad_ref[...] = jnp.sum(total * proj_ref[...].astype(F32), axis=0, keepdims=True)


def local(groups, mates, axes, queries, keys, values, out_grad, pair, ln_gain, proj_weight, token_mask, atom_map):
    _, width, count = queries.shape
    rows, cols, chan = pair.shape
    heads = proj_weight.shape[1]
    dim = width // mates
    head_parts = heads // mates
    devices = groups * mates * head_parts
    entries = rows * cols
    half = rows // 2
    gain_row = ln_gain.reshape(1, chan)
    proj_rows = proj_weight.T
    mask_row = token_mask.reshape(1, count)
    pair = pair.reshape(2, half, cols, chan)
    mate = lax.axis_index(axes[1]).astype(jnp.int32).reshape(1)
    whole = lambda *shape: pl.BlockSpec(shape, lambda *_: (0,) * len(shape))
    scalar = pl.BlockSpec(memory_space=pltpu.SMEM)
    vector = pl.BlockSpec(memory_space=pltpu.VMEM)

    def swap(chunks):
        return [
            lax.ppermute(x, axes[1], [(i, i ^ k) for i in range(mates)]) if k else x
            for k, x in enumerate(chunks)
        ]

    block = step_of(half, 16)
    far = pl.BlockSpec(memory_space=pltpu.HBM)
    tiles = jax.ShapeDtypeStruct((devices, cols, rows), BF16)
    by_head = pltpu.VMEM(((heads + 1) * half, 2 * cols), F32)
    near = pltpu.VMEM(pair.shape, BF16)
    sems = pltpu.SemaphoreType.DMA((half // block,))

    chunks = (jax.ShapeDtypeStruct((4 * dim, count), BF16),) * mates
    send = call(
        functools.partial(pack_kernel, dim), "pack", 0, 16 * width * count, SMALL,
        out_shape=chunks,
        in_specs=[scalar] + [far] * 4,
        out_specs=(vector,) * mates,
        scratch_shapes=[pltpu.SemaphoreType.DMA((mates, 4))],
    )(mate, queries, keys, values, out_grad)
    got = swap(send)

    bias_send = call(
        functools.partial(norm_kernel, groups, mates, block), "norm", 2 * entries * chan * heads,
        2 * entries * chan, BIG,
        out_shape=tiles,
        in_specs=[vector] * 3,
        out_specs=vector,
        scratch_shapes=[by_head],
    )(pair, gain_row, proj_rows)
    bias = lax.all_to_all(bias_send, axes, 0, 0, tiled=True)

    weight = call(
        weight_kernel, "weight", 2 * 144 * atom_map.shape[0], 0, SMALL,
        out_shape=jax.ShapeDtypeStruct((1, count), F32),
    )(atom_map.reshape(1, -1), mask_row)

    fine = rows % 128 == 0
    samp = groups * mates
    bias = bias.reshape(samp, head_parts, cols, rows)
    if not fine:
        bias = bias.transpose(0, 2, 1, 3).reshape(1, 1, count, count)
    wide = max(rows, step_of(count, 512)) if fine else count
    order = sorted(range(mates), key=lambda k: ORDER.index(k) if k in ORDER else k)
    back, before = [None] * mates, ()
    for n in range(0, mates, SPLIT):
        part = order[n : n + SPLIT]
        many, last = len(part), n + SPLIT >= mates
        *outs, grads = call(
            functools.partial(attend_kernel, many, wide, last), "attend", 12 * many * dim * count * count,
            8 * many * dim * count * 2 + 4 * count * count, SMALL,
            out_shape=chunks[:many]
            + (jax.ShapeDtypeStruct(bias.shape, BF16) if last else jax.ShapeDtypeStruct((count, count), F32),),
            scratch_shapes=[
                pltpu.VMEM((many, count, 2 * dim + 16), BF16),
                pltpu.VMEM((many, count, dim), BF16),
                pltpu.VMEM((many, dim, count), F32),
                pltpu.VMEM((many, dim, count), F32),
            ],
        )(*[got[k] for k in part], bias, mask_row, weight, *before)
        before = (grads,)
        for k, x in zip(part, outs):
            back[k] = x
    if not fine:
        grads = grads.reshape(samp, cols, head_parts, rows).transpose(0, 2, 1, 3)
    swapped = swap(back)
    pair_later, swapped = together(pair, swapped, NEXT)
    inv_std = call(
        functools.partial(prepare_kernel, block), "prepare", 2 * entries * chan * heads, 2 * entries * chan, SMALL,
        out_shape=jax.ShapeDtypeStruct((cols, rows), F32),
        in_specs=[vector],
        out_specs=vector,
        scratch_shapes=[pltpu.VMEM((half, 2 * cols), F32)],
    )(pair_later)
    grads, swapped = together(grads, swapped, FIRST)
    grads = lax.all_to_all(grads.reshape(devices, cols, rows), axes, 0, 0, tiled=True)
    parts = call(
        functools.partial(reduce_kernel, groups, mates), "reduce", 2 * entries * chan * heads,
        2 * entries * chan, SMALL,
        out_shape=jax.ShapeDtypeStruct((devices, heads, chan), BF16),
        in_specs=[vector] * 3,
        out_specs=vector,
        scratch_shapes=[by_head],
    )(grads, inv_std, pair)
    parts, swapped = together(parts, swapped, EARLY)
    sums = lax.all_to_all(parts, axes, 0, 0, tiled=True)

    early, late = [k for k in range(mates) if k not in LATE], [k for k in LATE if k < mates]
    whole_outs = (jax.ShapeDtypeStruct(queries.shape, BF16),) * 4
    pair_grad, *wholes = call(
        functools.partial(pair_kernel, groups, mates, block, early, dim), "pair_grad", 8 * entries * chan * heads,
        4 * entries * chan, SMALL,
        out_shape=(jax.ShapeDtypeStruct(pair.shape, BF16),) + whole_outs,
        in_specs=[scalar] + [vector] * (len(early) + 6),
        out_specs=(far,) * 5,
        scratch_shapes=[near, sems, by_head, by_head, pltpu.SemaphoreType.DMA((len(early), 4))],
    )(mate, *[swapped[k] for k in early], grads, bias_send, inv_std, gain_row, proj_rows, pair)
    pair_grad, swapped = together(pair_grad, swapped, LATE)
    if late:
        wholes = call(
            functools.partial(unpack_kernel, late, dim), "unpack", 0, 16 * width * count, SMALL,
            out_shape=whole_outs,
            in_specs=[scalar] + [vector] * len(late) + [far] * 4,
            out_specs=(far,) * 4,
            scratch_shapes=[pltpu.SemaphoreType.DMA((len(late), 4))],
            input_output_aliases={1 + len(late) + n: n for n in range(4)},
        )(mate, *[swapped[k] for k in late], *wholes)
    attended, query_grad, key_grad, value_grad = wholes
    weight_rows, gain_grad = call(
        functools.partial(final_kernel, 1.0 / count), "final", 0, 2 * devices * heads * chan, SMALL,
        out_shape=(
            jax.ShapeDtypeStruct((heads, chan), F32),
            jax.ShapeDtypeStruct((1, chan), F32),
        ),
    )(sums, gain_row, proj_rows)
    return (
        attended, query_grad, key_grad, value_grad,
        pair_grad.reshape(rows, cols, chan), weight_rows.T, gain_grad.reshape(chan),
    )


def solution(mesh):
    samp, head = mesh.axis_names
    samp_size, head_size = mesh.shape[samp], mesh.shape[head]

    def run(*args):
        heads = args[6].shape[1]
        mates = math.gcd(heads // head_size, samp_size)
        groups = samp_size // mates
        axes = ("group", "mate", "part")
        fine = Mesh(mesh.devices.reshape(groups, mates, head_size), axes)
        by_sample = P(("group", "mate"), "part", None)
        by_pair = P("part", ("group", "mate"), None)
        return jax.shard_map(
            functools.partial(local, groups, mates, axes),
            mesh=fine,
            in_specs=(by_sample,) * 4 + (by_pair,) + (P(),) * 4,
            out_specs=(by_sample,) * 4 + (by_pair, P(), P()),
            check_vma=False,
        )(*args)

    return run
```
